1024 devices in a mesh: expert: 64 (over y_hi, x, core), dp: 16 (over y_lo, z).
Axes of the slice: x: 8, y: 8 (y_hi: 4, y_lo: 2; y = y_hi * 2 + y_lo), z: 8, core: 2. Of those that a mesh axis runs over, the one named last changes fastest.
Arguments:
- tokens: bfloat16 [131072, 2048], P(('expert', 'dp')), may hold values from -6 to 6
- cotangent: bfloat16 [131072, 2048], P(('expert', 'dp')), may hold values from -1.5 to 1.5
- gate_scores: bfloat16 [131072], P(('expert', 'dp')), may hold values from 0.19921875 to 1
- expert_ids: int32 [131072], P(('expert', 'dp')), may hold values from 0 to 63, as said below
- slot_index: int32 [131072], P(('expert', 'dp')), may hold values from 0 to 3, as said below
- gate_weight: bfloat16 [64, 2048, 384], P('expert'), may hold values from -0.125 to 0.125
- up_weight: bfloat16 [64, 2048, 384], P('expert'), may hold values from -0.125 to 0.125
- down_weight: bfloat16 [64, 384, 2048], P('expert'), may hold values from -0.3125 to 0.3125
Outputs:
- token_grad: bfloat16 [131072, 2048], P(('expert', 'dp'))
- score_grad: bfloat16 [131072], P(('expert', 'dp'))
- grad_gate: bfloat16 [64, 2048, 384], P('expert', 'dp')
- grad_up: bfloat16 [64, 2048, 384], P('expert', 'dp')
- grad_down: bfloat16 [64, 384, 2048], P('expert', None, 'dp')
The draws below stay inside these ranges and needn't reach their ends.
Inputs may be any that keep to these rules, and one draw needn't show every extreme that they name: `expert_ids`: within the 128 tokens of one device no expert is named more than 4 times, and some expert exactly 4 times. `slot_index`: tokens of one device with the same expert have distinct slots.
All inputs are finite; a program needn't handle non-finite values.
Results may differ from the reference program's by a relative error of at most 0.024.
Values may be sent and summed in bfloat16 or wider, within the bound.
No kernel may reach another device: no remote copies, remote signals or barrier semaphores. Data moves between devices by JAX's collectives and lax.ppermute only.
A program may use at most 64 MiB of HBM per device.

```python
import jax
import jax.numpy as jnp
from jax import lax

D = 2048
H = 384
TOK_DEV = 128
EXPERTS = 64
GROUPS = 16
CAP = 4
TOKENS = 131072


def routing(key):
    blocks = TOKENS // TOK_DEV
    keys = jax.random.split(key, blocks)

    def one_block(block_key):
        first_key, second_key, third_key = jax.random.split(block_key, 3)
        ordering = jax.random.permutation(first_key, EXPERTS * CAP).astype(jnp.int32)
        filled = jax.random.randint(second_key, (), 0, EXPERTS).astype(jnp.int32)
        rank_key = jnp.where(ordering // CAP == filled, 0, 1).astype(jnp.int32)
        arranged = ordering[jnp.argsort(rank_key, stable=True)]
        chosen = arranged[:TOK_DEV]
        return jax.random.permutation(third_key, chosen)
    picks = jax.vmap(one_block)(keys).reshape(-1).astype(jnp.int32)
    return (picks // CAP, picks % CAP)


def draw_expert_ids(key, part):
    return routing(key)[0]


def draw_slot_index(key, part):
    return routing(key)[1]


def level_of(own_key, dims, pieces, low, largest):
    gain = 1.0
    for dim, blocks in pieces:
        heights = jax.random.uniform(jax.random.fold_in(jax.random.fold_in(own_key, 6), dim), (blocks,), jnp.float32, low / len(pieces), largest / len(pieces))
        gain = gain * jnp.repeat(jnp.exp(heights), dims[dim] // blocks).reshape((-1,) + (1,) * (len(dims) - 1 - dim))
    return gain


def centred(key, dims, scale, limit, pieces=(), held_as=jnp.bfloat16):
    drawn = scale * jax.random.normal(key, dims, jnp.float32)
    if pieces:
        drawn = drawn * level_of(key, dims, pieces, -0.22, 0.18)
    return jnp.clip(drawn, -limit, limit).astype(held_as)


def setup_inputs(seed: int = 0) -> dict:
    arg_keys = jax.random.split(jax.random.key(seed), 9)
    tokens = centred(arg_keys[0], (TOKENS, D), 1.0, 6.0, ((0, 1024),))
    cotangent = centred(arg_keys[1], (TOKENS, D), 0.25, 1.5, ((0, 1024),))
    gate_scores = jnp.clip(0.19921875 + 0.80078125 * jax.random.uniform(arg_keys[2], (TOKENS,), jnp.float32) ** level_of(arg_keys[2], (TOKENS,), ((0, 1024),), -0.2, 0.2), 0.19921875, 1.0).astype(jnp.bfloat16)
    expert_ids = draw_expert_ids(jax.random.fold_in(arg_keys[8], 71), 0)
    slot_index = draw_slot_index(jax.random.fold_in(arg_keys[8], 71), 0)
    gate_weight = centred(arg_keys[5], (EXPERTS, D, H), D ** -0.5, 0.125, ((0, 64),))
    up_weight = centred(arg_keys[6], (EXPERTS, D, H), D ** -0.5, 0.125, ((0, 64),))
    down_weight = centred(arg_keys[7], (EXPERTS, H, D), H ** -0.5, 0.3125, ((0, 64),))
    return dict(tokens=tokens, cotangent=cotangent, gate_scores=gate_scores, expert_ids=expert_ids, slot_index=slot_index, gate_weight=gate_weight, up_weight=up_weight, down_weight=down_weight)


def silu_parts(pre_gate):
    sigmoid = jax.nn.sigmoid(pre_gate)
    return sigmoid, pre_gate * sigmoid


def expert_pass(packed):
    inputs, cotan_rows, score_rows, gate_matrix, up_matrix, down_matrix = packed
    inputs_float = inputs.astype(jnp.float32)
    gate_float = gate_matrix.astype(jnp.float32)
    up_float = up_matrix.astype(jnp.float32)
    down_float = down_matrix.astype(jnp.float32)
    pre_gate = jnp.einsum("grd,dh->grh", inputs_float, gate_float)
    pre_up = jnp.einsum("grd,dh->grh", inputs_float, up_float)
    sigmoid, activated = silu_parts(pre_gate)
    hidden = (activated * pre_up).astype(jnp.bfloat16)
    hidden_float = hidden.astype(jnp.float32)
    output = jnp.einsum("grh,hd->grd", hidden_float, down_float)
    cotan_float = cotan_rows.astype(jnp.float32)
    slot_score = jnp.sum(cotan_float * output, axis=2).astype(jnp.bfloat16)
    scaled = (score_rows.astype(jnp.float32)[:, :, None] * cotan_float).astype(jnp.bfloat16)
    scaled_float = scaled.astype(jnp.float32)
    hidden_grad = jnp.einsum("grd,hd->grh", scaled_float, down_float)
    up_grad = (hidden_grad * activated).astype(jnp.bfloat16).astype(jnp.float32)
    pre_grad = (hidden_grad * pre_up * sigmoid * (1.0 + pre_gate * (1.0 - sigmoid))).astype(jnp.bfloat16).astype(jnp.float32)
    input_grad = (jnp.einsum("grh,dh->grd", pre_grad, gate_float) + jnp.einsum("grh,dh->grd", up_grad, up_float)).astype(jnp.bfloat16)
    part_gate = jnp.einsum("grd,grh->gdh", inputs_float, pre_grad).astype(jnp.bfloat16)
    part_up = jnp.einsum("grd,grh->gdh", inputs_float, up_grad).astype(jnp.bfloat16)
    part_down = jnp.einsum("grh,grd->ghd", hidden_float, scaled_float).astype(jnp.bfloat16)
    grad_gate = jnp.sum(part_gate.astype(jnp.float32), axis=0).astype(jnp.bfloat16)
    grad_up = jnp.sum(part_up.astype(jnp.float32), axis=0).astype(jnp.bfloat16)
    grad_down = jnp.sum(part_down.astype(jnp.float32), axis=0).astype(jnp.bfloat16)
    return input_grad, slot_score, grad_gate, grad_up, grad_down


def reference(tokens, cotangent, gate_scores, expert_ids, slot_index, gate_weight, up_weight, down_weight):
    block = jnp.arange(TOKENS, dtype=jnp.int32) // TOK_DEV
    group = block % GROUPS
    source = block // GROUPS
    per_group = EXPERTS * CAP
    per_expert = GROUPS * per_group
    destination = (expert_ids * per_expert + group * per_group + source * CAP + slot_index).astype(jnp.int32)
    total = EXPERTS * per_expert
    inputs = jnp.zeros((total, D), tokens.dtype).at[destination].set(tokens).reshape(EXPERTS, GROUPS, per_group, D)
    cotan = jnp.zeros((total, D), cotangent.dtype).at[destination].set(cotangent).reshape(EXPERTS, GROUPS, per_group, D)
    scores = jnp.zeros((total,), gate_scores.dtype).at[destination].set(gate_scores).reshape(EXPERTS, GROUPS, per_group)
    input_grad, slot_score, grad_gate, grad_up, grad_down = lax.map(expert_pass, (inputs, cotan, scores, gate_weight, up_weight, down_weight))
    token_grad = input_grad.reshape(total, D)[destination]
    score_grad = slot_score.reshape(total)[destination]
    return token_grad, score_grad, grad_gate, grad_up, grad_down
```

```python
import functools

import jax
import jax.numpy as jnp
from jax import lax
from jax.experimental import pallas as pl
from jax.experimental.pallas import tpu as pltpu
from jax.sharding import PartitionSpec as P

F32 = jnp.float32
BF16 = jnp.bfloat16
LANES = 128


def dot(left, right, left_dim, right_dim):
    return lax.dot_general(
        left, right, (((left_dim,), (right_dim,)), ((), ())), preferred_element_type=F32
    )


def dispatch_kernel(capacity, ids_ref, slot_ref, score_ref, tokens_ref, cotan_ref, out_ref):
    rows, count = out_ref.shape[0], tokens_ref.shape[0]
    position = ids_ref[...] * (2 * capacity) + slot_ref[...]
    row = lax.broadcasted_iota(jnp.int32, (rows, count), 0)
    pick_token = jnp.where(row == position, F32(1), F32(0)).astype(BF16)
    pick_cotan = jnp.where(
        row == position + capacity, score_ref[...].astype(F32), F32(0)
    ).astype(BF16)
    out_ref[...] = (
        dot(pick_token, tokens_ref[...], 1, 0) + dot(pick_cotan, cotan_ref[...], 1, 0)
    ).astype(BF16)


def dispatch(expert_ids, slot_index, gate_scores, tokens, cotangent, experts, capacity):
    count, features = tokens.shape
    rows = experts * 2 * capacity
    block = min(512, features)
    small = pl.BlockSpec((1, count), lambda i: (0, 0))
    wide = pl.BlockSpec((count, block), lambda i: (0, i))
    return pl.pallas_call(
        functools.partial(dispatch_kernel, capacity),
        grid=(features // block,),
        in_specs=[small, small, small, wide, wide],
        out_specs=pl.BlockSpec((rows, block), lambda i: (0, i)),
        out_shape=jax.ShapeDtypeStruct((rows, features), BF16),
        compiler_params=pltpu.CompilerParams(vmem_limit_bytes=24 * 2**20),
        name="dispatch",
    )(
        expert_ids.reshape(1, count),
        slot_index.reshape(1, count),
        gate_scores.reshape(1, count),
        tokens,
        cotangent,
    )


def pick_rows(slots, rows, capacity, half):
    slot = lax.broadcasted_iota(jnp.int32, (slots, rows), 0)
    row = lax.broadcasted_iota(jnp.int32, (slots, rows), 1)
    wanted = (slot // capacity) * (2 * capacity) + slot % capacity + half * capacity
    return jnp.where(row == wanted, F32(1), F32(0)).astype(BF16)


def expert_kernel(
    capacity, recv_ref, gate_ref, up_ref, down_ref, grads_ref, inner_ref, score_ref,
    inputs, scaled, hidden_sc, inner_sc,
):
    rows = recv_ref.shape[0]
    slots = rows // 2
    hidden_size = gate_ref.shape[1]
    block = grads_ref.shape[0]
    step = pl.program_id(0)

    @pl.when(step == 0)
    def _():
        received = recv_ref[...]
        inputs[...] = dot(pick_rows(slots, rows, capacity, 0), received, 1, 0).astype(BF16)
        scaled[...] = dot(pick_rows(slots, rows, capacity, 1), received, 1, 0).astype(BF16)
        pre_gate = dot(inputs[...], gate_ref[...], 1, 0)
        pre_up = dot(inputs[...], up_ref[...], 1, 0)
        hidden_grad = dot(scaled[...], down_ref[...], 1, 1)
        sigmoid = jax.nn.sigmoid(pre_gate)
        activated = pre_gate * sigmoid
        hidden = (activated * pre_up).astype(BF16)
        hidden_sc[...] = hidden
        inner_sc[:, :hidden_size] = (
            hidden_grad * pre_up * sigmoid * (1.0 + pre_gate * (1.0 - sigmoid))
        ).astype(BF16)
        inner_sc[:, hidden_size:] = (hidden_grad * activated).astype(BF16)
        inner_ref[...] = inner_sc[...]
        score = jnp.sum(hidden.astype(F32) * hidden_grad, axis=1, keepdims=True)
        score_ref[...] = jnp.broadcast_to(score, score_ref.shape).astype(BF16)

    columns = pl.ds(pl.multiple_of(step * block, block), block)
    grads_ref[:, : 2 * hidden_size] = dot(inputs[:, columns], inner_sc[...], 0, 0).astype(BF16)
    grads_ref[:, 2 * hidden_size :] = dot(scaled[:, columns], hidden_sc[...], 0, 0).astype(BF16)


def expert_grads(received, gate, up, down, capacity):
    rows, features = received.shape
    hidden_size = gate.shape[1]
    slots = rows // 2
    block = min(256, features)
    whole = lambda shape: pl.BlockSpec(shape, lambda i: (0, 0))
    return pl.pallas_call(
        functools.partial(expert_kernel, capacity),
        grid=(features // block,),
        in_specs=[whole(received.shape), whole(gate.shape), whole(up.shape), whole(down.shape)],
        out_specs=[
            pl.BlockSpec((block, 3 * hidden_size), lambda i: (i, 0)),
            whole((slots, 2 * hidden_size)),
            whole((slots, LANES)),
        ],
        out_shape=[
            jax.ShapeDtypeStruct((features, 3 * hidden_size), BF16),
            jax.ShapeDtypeStruct((slots, 2 * hidden_size), BF16),
            jax.ShapeDtypeStruct((slots, LANES), BF16),
        ],
        scratch_shapes=[
            pltpu.VMEM((slots, features), BF16),
            pltpu.VMEM((slots, features), BF16),
            pltpu.VMEM((slots, hidden_size), BF16),
            pltpu.VMEM((slots, 2 * hidden_size), BF16),
        ],
        compiler_params=pltpu.CompilerParams(vmem_limit_bytes=40 * 2**20),
        name="expert_grads",
    )(received, gate, up, down)


def return_kernel(capacity, inner_ref, score_ref, gate_ref, up_ref, out_ref):
    slots = inner_ref.shape[0]
    rows = out_ref.shape[0]
    hidden_size = gate_ref.shape[1]
    half = gate_ref.shape[0] // 2
    total = jnp.zeros((rows, half), F32)
    for part in range(2):
        piece = pl.ds(part * half, half)
        input_grad = dot(inner_ref[:, :hidden_size], gate_ref[piece, :], 1, 1) + dot(
            inner_ref[:, hidden_size:], up_ref[piece, :], 1, 1
        )
        spread = pick_rows(slots, rows, capacity, part)
        total += dot(spread, input_grad.astype(BF16), 0, 0)
        if part == 0:
            out_ref[:, half:] = dot(spread, score_ref[...], 0, 0).astype(BF16)
    out_ref[:, :half] = total.astype(BF16)


def return_rows(inner, score, gate, up, capacity):
    slots = inner.shape[0]
    half = gate.shape[0] // 2
    return pl.pallas_call(
        functools.partial(return_kernel, capacity),
        out_shape=jax.ShapeDtypeStruct((2 * slots, half + LANES), BF16),
        compiler_params=pltpu.CompilerParams(vmem_limit_bytes=40 * 2**20),
        name="return_rows",
    )(inner, score, gate, up)


def combine_kernel(capacity, ids_ref, slot_ref, score_ref, rows_ref, token_ref, grad_ref):
    rows = rows_ref.shape[0]
    count = token_ref.shape[0]
    half = token_ref.shape[1] // 2
    position = ids_ref[...] * (2 * capacity) + slot_ref[...]
    row = lax.broadcasted_iota(jnp.int32, (rows, count), 0)
    for part in range(2):
        pick = jnp.where(row == position + part * capacity, F32(1), F32(0)).astype(BF16)
        token_ref[:, part * half : (part + 1) * half] = dot(
            pick, rows_ref[:, :half], 0, 0
        ).astype(BF16)
        if part == 0:
            score = dot(rows_ref[:, half:], pick, 0, 0)
            grad_ref[...] = (score[0:1, :] / score_ref[...].astype(F32)).astype(BF16)


def combine(expert_ids, slot_index, gate_scores, rows, features, capacity):
    count = expert_ids.shape[0]
    return pl.pallas_call(
        functools.partial(combine_kernel, capacity),
        out_shape=[
            jax.ShapeDtypeStruct((count, features), BF16),
            jax.ShapeDtypeStruct((1, count), BF16),
        ],
        compiler_params=pltpu.CompilerParams(vmem_limit_bytes=24 * 2**20),
        name="combine",
    )(
        expert_ids.reshape(1, count),
        slot_index.reshape(1, count),
        gate_scores.reshape(1, count),
        rows,
    )


def split_kernel(summed_ref, gate_ref, up_ref, down_ref):
    hidden_size = gate_ref.shape[1]
    gate_ref[...] = summed_ref[:, :hidden_size]
    up_ref[...] = summed_ref[:, hidden_size : 2 * hidden_size]
    down_ref[...] = summed_ref[:, 2 * hidden_size :].astype(F32).T.astype(BF16)


def split_grads(summed):
    block, width = summed.shape
    hidden_size = width // 3
    return pl.pallas_call(
        split_kernel,
        out_shape=[
            jax.ShapeDtypeStruct((block, hidden_size), BF16),
            jax.ShapeDtypeStruct((block, hidden_size), BF16),
            jax.ShapeDtypeStruct((hidden_size, block), BF16),
        ],
        name="split_grads",
    )(summed)


def on_device(
    tokens, cotangent, gate_scores, expert_ids, slot_index, gate_weight, up_weight, down_weight
):
    experts = lax.axis_size("expert")
    count, features = tokens.shape
    capacity = 2 * count // experts
    gate, up, down = gate_weight[0], up_weight[0], down_weight[0]
    send = dispatch(expert_ids, slot_index, gate_scores, tokens, cotangent, experts, capacity)
    received = lax.all_to_all(
        send.reshape(experts, 2 * capacity, features),
        "expert", split_axis=0, concat_axis=0, tiled=True,
    ).reshape(send.shape)
    grads, inner, score = expert_grads(received, gate, up, down, capacity)
    summed = lax.psum_scatter(grads, "dp", scatter_dimension=0, tiled=True)
    back = return_rows(inner, score, gate, up, capacity)
    returned = lax.all_to_all(
        back.reshape(experts, 2 * capacity, back.shape[1]),
        "expert", split_axis=0, concat_axis=0, tiled=True,
    ).reshape(back.shape)
    token_grad, score_grad = combine(
        expert_ids, slot_index, gate_scores, returned, features, capacity
    )
    grad_gate, grad_up, grad_down = split_grads(summed)
    return token_grad, score_grad.reshape(count), grad_gate[None], grad_up[None], grad_down[None]


def solution(mesh):
    both = ("expert", "dp")
    return jax.shard_map(
        on_device,
        mesh=mesh,
        in_specs=(
            P(both, None),
            P(both, None),
            P(both),
            P(both),
            P(both),
            P("expert", None, None),
            P("expert", None, None),
            P("expert", None, None),
        ),
        out_specs=(
            P(both, None),
            P(both),
            P("expert", "dp", None),
            P("expert", "dp", None),
            P("expert", None, "dp"),
        ),
        check_vma=False,
    )
```

```python
import functools

import jax
import jax.numpy as jnp
from jax import lax
from jax.experimental import pallas as pl
from jax.experimental.pallas import tpu as pltpu
from jax.sharding import PartitionSpec as P

F32 = jnp.float32
BF16 = jnp.bfloat16
LANES = 128


def dot(left, right, left_dim, right_dim):
    return lax.dot_general(
        left, right, (((left_dim,), (right_dim,)), ((), ())), preferred_element_type=F32
    )


def dispatch_kernel(capacity, ids_ref, slot_ref, score_ref, tokens_ref, cotan_ref, out_ref):
    rows, count = out_ref.shape[0], tokens_ref.shape[0]
    position = ids_ref[...] * (2 * capacity) + slot_ref[...]
    row = lax.broadcasted_iota(jnp.int32, (rows, count), 0)
    pick_token = jnp.where(row == position, F32(1), F32(0)).astype(BF16)
    pick_cotan = jnp.where(
        row == position + capacity, score_ref[...].astype(F32), F32(0)
    ).astype(BF16)
    out_ref[...] = (
        dot(pick_token, tokens_ref[...], 1, 0) + dot(pick_cotan, cotan_ref[...], 1, 0)
    ).astype(BF16)


def dispatch(expert_ids, slot_index, gate_scores, tokens, cotangent, experts, capacity):
    count, features = tokens.shape
    rows = experts * 2 * capacity
    block = min(512, features)
    small = pl.BlockSpec((1, count), lambda i: (0, 0))
    wide = pl.BlockSpec((count, block), lambda i: (0, i))
    return pl.pallas_call(
        functools.partial(dispatch_kernel, capacity),
        grid=(features // block,),
        in_specs=[small, small, small, wide, wide],
        out_specs=pl.BlockSpec((rows, block), lambda i: (0, i)),
        out_shape=jax.ShapeDtypeStruct((rows, features), BF16),
        compiler_params=pltpu.CompilerParams(vmem_limit_bytes=60 * 2**20),
        name="dispatch",
    )(
        expert_ids.reshape(1, count),
        slot_index.reshape(1, count),
        gate_scores.reshape(1, count),
        tokens,
        cotangent,
    )


def pick_rows(slots, rows, capacity, half):
    slot = lax.broadcasted_iota(jnp.int32, (slots, rows), 0)
    row = lax.broadcasted_iota(jnp.int32, (slots, rows), 1)
    wanted = (slot // capacity) * (2 * capacity) + slot % capacity + half * capacity
    return jnp.where(row == wanted, F32(1), F32(0)).astype(BF16)


def expert_kernel(
    capacity, side_ref, recv_ref, gate_ref, up_ref, down_ref, grads_ref, inner_ref, score_ref,
    inputs, scaled, hidden_sc, inner_sc,
):
    rows = recv_ref.shape[0]
    slots = rows // 2
    hidden_size = gate_ref.shape[1]
    block = grads_ref.shape[0] // 2
    step = pl.program_id(0)
    side = side_ref[0]

    @pl.when(step == 0)
    def _():
        received = recv_ref[...]
        inputs[...] = dot(pick_rows(slots, rows, capacity, 0), received, 1, 0).astype(BF16)
        scaled[...] = dot(pick_rows(slots, rows, capacity, 1), received, 1, 0).astype(BF16)
        pre_gate = dot(inputs[...], gate_ref[...], 1, 0)
        pre_up = dot(inputs[...], up_ref[...], 1, 0)
        hidden_grad = dot(scaled[...], down_ref[...], 1, 1)
        sigmoid = jax.nn.sigmoid(pre_gate)
        activated = pre_gate * sigmoid
        hidden = (activated * pre_up).astype(BF16)
        hidden_sc[...] = hidden
        inner_sc[:, :hidden_size] = (
            hidden_grad * pre_up * sigmoid * (1.0 + pre_gate * (1.0 - sigmoid))
        ).astype(BF16)
        inner_sc[:, hidden_size:] = (hidden_grad * activated).astype(BF16)
        inner_ref[...] = inner_sc[...]
        score = jnp.sum(hidden.astype(F32) * hidden_grad, axis=1, keepdims=True)
        score_ref[...] = jnp.broadcast_to(score, score_ref.shape).astype(BF16)

    for piece in range(2):
        owner = side if piece else 1 - side
        first = (owner * pl.num_programs(0) + step) * block
        columns = pl.ds(pl.multiple_of(first, block), block)
        rows_out = slice(piece * block, (piece + 1) * block)
        grads_ref[rows_out, : 2 * hidden_size] = dot(
            inputs[:, columns], inner_sc[...], 0, 0
        ).astype(BF16)
        grads_ref[rows_out, 2 * hidden_size :] = dot(
            scaled[:, columns], hidden_sc[...], 0, 0
        ).astype(BF16)


def expert_grads(side, ring, received, gate, up, down, capacity):
    rows, features = received.shape
    hidden_size = gate.shape[1]
    slots = rows // 2
    block = features // ring
    whole = lambda shape: pl.BlockSpec(shape, lambda i, side: (0, 0))
    return pl.pallas_call(
        functools.partial(expert_kernel, capacity),
        grid_spec=pltpu.PrefetchScalarGridSpec(
            num_scalar_prefetch=1,
            grid=(ring,),
            in_specs=[whole(received.shape), whole(gate.shape), whole(up.shape), whole(down.shape)],
            out_specs=[
                pl.BlockSpec((block, 3 * hidden_size), lambda i, side: (i, 0)),
                whole((slots, 2 * hidden_size)),
                whole((slots, LANES)),
            ],
            scratch_shapes=[
                pltpu.VMEM((slots, features), BF16),
                pltpu.VMEM((slots, features), BF16),
                pltpu.VMEM((slots, hidden_size), BF16),
                pltpu.VMEM((slots, 2 * hidden_size), BF16),
            ],
        ),
        out_shape=[
            pltpu.HBM((features, 3 * hidden_size), BF16),
            jax.ShapeDtypeStruct((slots, 2 * hidden_size), BF16),
            jax.ShapeDtypeStruct((slots, LANES), BF16),
        ],
        compiler_params=pltpu.CompilerParams(vmem_limit_bytes=40 * 2**20),
        name="expert_grads",
    )(side, received, gate, up, down)


def return_kernel(capacity, inner_ref, score_ref, gate_ref, up_ref, out_ref):
    slots = inner_ref.shape[0]
    rows = out_ref.shape[0]
    hidden_size = gate_ref.shape[1]
    half = gate_ref.shape[0] // 2
    total = jnp.zeros((rows, half), F32)
    for part in range(2):
        piece = pl.ds(part * half, half)
        input_grad = dot(inner_ref[:, :hidden_size], gate_ref[piece, :], 1, 1) + dot(
            inner_ref[:, hidden_size:], up_ref[piece, :], 1, 1
        )
        spread = pick_rows(slots, rows, capacity, part)
        total += dot(spread, input_grad.astype(BF16), 0, 0)
        if part == 0:
            out_ref[:, half:] = dot(spread, score_ref[...], 0, 0).astype(BF16)
    out_ref[:, :half] = total.astype(BF16)


def return_rows(inner, score, gate, up, capacity):
    slots = inner.shape[0]
    half = gate.shape[0] // 2
    return pl.pallas_call(
        functools.partial(return_kernel, capacity),
        out_shape=jax.ShapeDtypeStruct((2 * slots, half + LANES), BF16),
        compiler_params=pltpu.CompilerParams(vmem_limit_bytes=40 * 2**20),
        name="return_rows",
    )(inner, score, gate, up)


def combine_kernel(capacity, ids_ref, slot_ref, score_ref, rows_ref, token_ref, grad_ref):
    rows = rows_ref.shape[0]
    count = token_ref.shape[0]
    half = token_ref.shape[1] // 2
    position = ids_ref[...] * (2 * capacity) + slot_ref[...]
    row = lax.broadcasted_iota(jnp.int32, (rows, count), 0)
    for part in range(2):
        pick = jnp.where(row == position + part * capacity, F32(1), F32(0)).astype(BF16)
        token_ref[:, part * half : (part + 1) * half] = dot(
            pick, rows_ref[:, :half], 0, 0
        ).astype(BF16)
        if part == 0:
            score = dot(rows_ref[:, half:], pick, 0, 0)
            grad_ref[...] = (score[0:1, :] / score_ref[...].astype(F32)).astype(BF16)


def combine(expert_ids, slot_index, gate_scores, rows, features, capacity):
    count = expert_ids.shape[0]
    return pl.pallas_call(
        functools.partial(combine_kernel, capacity),
        out_shape=[
            jax.ShapeDtypeStruct((count, features), BF16),
            jax.ShapeDtypeStruct((1, count), BF16),
        ],
        compiler_params=pltpu.CompilerParams(vmem_limit_bytes=24 * 2**20),
        name="combine",
    )(
        expert_ids.reshape(1, count),
        slot_index.reshape(1, count),
        gate_scores.reshape(1, count),
        rows,
    )


def split_kernel(kept_ref, arrived_ref, gate_ref, up_ref, down_ref):
    hidden_size = gate_ref.shape[1]
    total = kept_ref[...].astype(F32) + arrived_ref[...].astype(F32)
    gate_ref[...] = total[:, :hidden_size].astype(BF16)
    up_ref[...] = total[:, hidden_size : 2 * hidden_size].astype(BF16)
    down_ref[...] = total[:, 2 * hidden_size :].T.astype(BF16)


def split_grads(summed, arrived):
    block, width = arrived.shape
    hidden_size = width // 3
    return pl.pallas_call(
        split_kernel,
        grid=(1,),
        in_specs=[
            pl.BlockSpec((block, width), lambda i: (1, 0)),
            pl.BlockSpec((block, width), lambda i: (0, 0)),
        ],
        out_specs=[
            pl.BlockSpec((block, hidden_size), lambda i: (0, 0)),
            pl.BlockSpec((block, hidden_size), lambda i: (0, 0)),
            pl.BlockSpec((hidden_size, block), lambda i: (0, 0)),
        ],
        out_shape=[
            jax.ShapeDtypeStruct((block, hidden_size), BF16),
            jax.ShapeDtypeStruct((block, hidden_size), BF16),
            jax.ShapeDtypeStruct((hidden_size, block), BF16),
        ],
        name="split_grads",
    )(summed, arrived)


def on_device(
    tokens, cotangent, gate_scores, expert_ids, slot_index, gate_weight, up_weight, down_weight
):
    experts = lax.axis_size("expert")
    count, features = tokens.shape
    capacity = 2 * count // experts
    gate, up, down = gate_weight[0], up_weight[0], down_weight[0]
    send = dispatch(expert_ids, slot_index, gate_scores, tokens, cotangent, experts, capacity)
    received = lax.all_to_all(
        send.reshape(experts, 2 * capacity, features),
        "expert", split_axis=0, concat_axis=0, tiled=True,
    ).reshape(send.shape)
    ring = lax.axis_size("dp") // 2
    side = (lax.axis_index("dp") >= ring).astype(jnp.int32).reshape(1)
    grads, inner, score = expert_grads(side, ring, received, gate, up, down, capacity)
    summed = lax.psum_scatter(
        grads, "dp", scatter_dimension=0, tiled=True,
        axis_index_groups=[[s * ring + i for i in range(ring)] for s in range(2)],
    )
    arrived = lax.ppermute(
        summed[: summed.shape[0] // 2], "dp", [(i, (i + ring) % (2 * ring)) for i in range(2 * ring)]
    )
    back = return_rows(inner, score, gate, up, capacity)
    returned = lax.all_to_all(
        back.reshape(experts, 2 * capacity, back.shape[1]),
        "expert", split_axis=0, concat_axis=0, tiled=True,
    ).reshape(back.shape)
    token_grad, score_grad = combine(
        expert_ids, slot_index, gate_scores, returned, features, capacity
    )
    grad_gate, grad_up, grad_down = split_grads(summed, arrived)
    return token_grad, score_grad.reshape(count), grad_gate[None], grad_up[None], grad_down[None]


def solution(mesh):
    both = ("expert", "dp")
    return jax.shard_map(
        on_device,
        mesh=mesh,
        in_specs=(
            P(both, None),
            P(both, None),
            P(both),
            P(both),
            P(both),
            P("expert", None, None),
            P("expert", None, None),
            P("expert", None, None),
        ),
        out_specs=(
            P(both, None),
            P(both),
            P("expert", "dp", None),
            P("expert", "dp", None),
            P("expert", None, "dp"),
        ),
        check_vma=False,
    )
```

```python
import functools

import jax
import jax.numpy as jnp
from jax import lax
from jax.experimental import pallas as pl
from jax.experimental.pallas import tpu as pltpu
from jax.sharding import PartitionSpec as P

F32 = jnp.float32
BF16 = jnp.bfloat16
LANES = 128


def dot(left, right, left_dim, right_dim):
    return lax.dot_general(
        left, right, (((left_dim,), (right_dim,)), ((), ())), preferred_element_type=F32
    )


def in_hbm(*arrays):
    return [pltpu.with_memory_space_constraint(array, pltpu.HBM) for array in arrays]


def on_chip(*arrays):
    return [pltpu.with_memory_space_constraint(array, pltpu.VMEM) for array in arrays]


ANYWHERE = pl.BlockSpec(memory_space=pltpu.HBM)
ON_CHIP = pl.BlockSpec(memory_space=pltpu.VMEM)
CHUNKS = 4


def dispatch_kernel(
    capacity, ids_hbm, slot_hbm, score_hbm, tokens_hbm, cotan_hbm, out_ref,
    ids_ref, slot_ref, score_ref, rows_ref, sems,
):
    rows, (count, features) = out_ref.shape[0], tokens_hbm.shape
    chunk = features // CHUNKS
    columns = [slice(i * chunk, (i + 1) * chunk) for i in range(CHUNKS)]
    copies = [
        pltpu.make_async_copy(ids_hbm, ids_ref, sems.at[0]),
        pltpu.make_async_copy(slot_hbm, slot_ref, sems.at[1]),
        pltpu.make_async_copy(score_hbm, score_ref, sems.at[2]),
    ]
    for i, c in enumerate(columns):
        copies += [
            pltpu.make_async_copy(tokens_hbm.at[:, c], rows_ref.at[:count, c], sems.at[3 + 2 * i]),
            pltpu.make_async_copy(cotan_hbm.at[:, c], rows_ref.at[count:, c], sems.at[4 + 2 * i]),
        ]
    for copy in copies:
        copy.start()
    for copy in copies[:3]:
        copy.wait()
    position = ids_ref[...] * (2 * capacity) + slot_ref[...]
    row = lax.broadcasted_iota(jnp.int32, (rows, count), 0)
    pick_token = jnp.where(row == position, F32(1), F32(0))
    pick_cotan = jnp.where(row == position + capacity, score_ref[...].astype(F32), F32(0))
    pick = jnp.concatenate([pick_token, pick_cotan], axis=1).astype(BF16)
    for i, c in enumerate(columns):
        copies[3 + 2 * i].wait()
        copies[4 + 2 * i].wait()
        out_ref[:, c] = dot(pick, rows_ref[:, c], 1, 0).astype(BF16)


def dispatch(expert_ids, slot_index, gate_scores, tokens, cotangent, experts, capacity):
    count, features = tokens.shape
    rows = experts * 2 * capacity
    return pl.pallas_call(
        functools.partial(dispatch_kernel, capacity),
        in_specs=[ANYWHERE] * 5,
        out_specs=ON_CHIP,
        out_shape=pltpu.VMEM((rows, features), BF16),
        scratch_shapes=[
            pltpu.VMEM((1, count), jnp.int32),
            pltpu.VMEM((1, count), jnp.int32),
            pltpu.VMEM((1, count), BF16),
            pltpu.VMEM((2 * count, features), BF16),
            pltpu.SemaphoreType.DMA((3 + 2 * CHUNKS,)),
        ],
        compiler_params=pltpu.CompilerParams(vmem_limit_bytes=24 * 2**20),
        name="dispatch",
    )(
        *in_hbm(
            expert_ids.reshape(1, count),
            slot_index.reshape(1, count),
            gate_scores.reshape(1, count),
            tokens,
            cotangent,
        )
    )


def pick_rows(slots, rows, capacity, half):
    slot = lax.broadcasted_iota(jnp.int32, (slots, rows), 0)
    row = lax.broadcasted_iota(jnp.int32, (slots, rows), 1)
    wanted = (slot // capacity) * (2 * capacity) + slot % capacity + half * capacity
    return jnp.where(row == wanted, F32(1), F32(0)).astype(BF16)


def expert_kernel(
    capacity, ring, side_ref, recv_ref, gate_hbm, up_hbm, down_hbm, grads_hbm, inner_ref, score_ref,
    gate_ref, up_ref, down_ref, inputs, scaled, hidden_sc, grads_ref, sems, out_sems,
):
    rows, features = recv_ref.shape
    slots = rows // 2
    hidden_size = gate_ref.shape[1]
    side = side_ref[0]
    copies = [
        pltpu.make_async_copy(source, target, sems.at[i])
        for i, (source, target) in enumerate(
            ((gate_hbm, gate_ref), (up_hbm, up_ref), (down_hbm, down_ref))
        )
    ]
    for copy in copies:
        copy.start()
    received = recv_ref[...]
    inputs[...] = dot(pick_rows(slots, rows, capacity, 0), received, 1, 0).astype(BF16)
    scaled[...] = dot(pick_rows(slots, rows, capacity, 1), received, 1, 0).astype(BF16)
    copies[0].wait()
    pre_gate = dot(inputs[...], gate_ref[...], 1, 0)
    copies[1].wait()
    pre_up = dot(inputs[...], up_ref[...], 1, 0)
    copies[2].wait()
    hidden_grad = dot(scaled[...], down_ref[...], 1, 1)
    sigmoid = jax.nn.sigmoid(pre_gate)
    activated = pre_gate * sigmoid
    hidden = (activated * pre_up).astype(BF16)
    hidden_sc[...] = hidden
    inner_ref[:, :hidden_size] = (
        hidden_grad * pre_up * sigmoid * (1.0 + pre_gate * (1.0 - sigmoid))
    ).astype(BF16)
    inner_ref[:, hidden_size:] = (hidden_grad * activated).astype(BF16)
    score = jnp.sum(hidden.astype(F32) * hidden_grad, axis=1, keepdims=True)
    score_ref[...] = jnp.broadcast_to(score, score_ref.shape).astype(BF16)

    block = features // (2 * ring)
    writes = []
    for step in range(ring):
        for piece in range(2):
            owner = side if piece else 1 - side
            columns = pl.ds(pl.multiple_of((owner * ring + step) * block, block), block)
            first = (2 * step + piece) * block
            grads_ref[first : first + block, : 2 * hidden_size] = dot(
                inputs[:, columns], inner_ref[...], 0, 0
            ).astype(BF16)
            grads_ref[first : first + block, 2 * hidden_size :] = dot(
                scaled[:, columns], hidden_sc[...], 0, 0
            ).astype(BF16)
        done = slice(2 * step * block, 2 * (step + 1) * block)
        writes.append(
            pltpu.make_async_copy(grads_ref.at[done], grads_hbm.at[done], out_sems.at[step])
        )
        writes[-1].start()
    for write in writes:
        write.wait()


def expert_grads(side, ring, received, gate, up, down, capacity):
    rows, features = received.shape
    hidden_size = gate.shape[1]
    slots = rows // 2
    return pl.pallas_call(
        functools.partial(expert_kernel, capacity, ring),
        in_specs=[pl.BlockSpec(memory_space=pltpu.SMEM), ON_CHIP, ANYWHERE, ANYWHERE, ANYWHERE],
        out_specs=[ANYWHERE, ON_CHIP, ON_CHIP],
        out_shape=[
            pltpu.HBM((features, 3 * hidden_size), BF16),
            pltpu.VMEM((slots, 2 * hidden_size), BF16),
            pltpu.VMEM((slots, LANES), BF16),
        ],
        scratch_shapes=[
            pltpu.VMEM(gate.shape, BF16),
            pltpu.VMEM(up.shape, BF16),
            pltpu.VMEM(down.shape, BF16),
            pltpu.VMEM((slots, features), BF16),
            pltpu.VMEM((slots, features), BF16),
            pltpu.VMEM((slots, hidden_size), BF16),
            pltpu.VMEM((features, 3 * hidden_size), BF16),
            pltpu.SemaphoreType.DMA((3,)),
            pltpu.SemaphoreType.DMA((ring,)),
        ],
        compiler_params=pltpu.CompilerParams(vmem_limit_bytes=40 * 2**20),
        name="expert_grads",
    )(side, *on_chip(received), *in_hbm(gate, up, down))


def return_kernel(capacity, inner_ref, score_ref, gate_ref, up_ref, out_ref):
    slots = inner_ref.shape[0]
    rows = out_ref.shape[0]
    hidden_size = gate_ref.shape[1]
    half = gate_ref.shape[0] // 2
    total = jnp.zeros((rows, half), F32)
    for part in range(2):
        piece = pl.ds(part * half, half)
        input_grad = dot(inner_ref[:, :hidden_size], gate_ref[piece, :], 1, 1) + dot(
            inner_ref[:, hidden_size:], up_ref[piece, :], 1, 1
        )
        spread = pick_rows(slots, rows, capacity, part)
        total += dot(spread, input_grad.astype(BF16), 0, 0)
        if part == 0:
            out_ref[:, half:] = dot(spread, score_ref[...], 0, 0).astype(BF16)
    out_ref[:, :half] = total.astype(BF16)


def return_rows(inner, score, gate, up, capacity):
    slots = inner.shape[0]
    half = gate.shape[0] // 2
    return pl.pallas_call(
        functools.partial(return_kernel, capacity),
        out_shape=jax.ShapeDtypeStruct((2 * slots, half + LANES), BF16),
        compiler_params=pltpu.CompilerParams(vmem_limit_bytes=40 * 2**20),
        name="return_rows",
    )(*on_chip(inner, score), gate, up)


def combine_kernel(capacity, ids_ref, slot_ref, score_ref, rows_ref, token_ref, grad_ref):
    rows = rows_ref.shape[0]
    count = token_ref.shape[0]
    half = token_ref.shape[1] // 2
    position = ids_ref[...] * (2 * capacity) + slot_ref[...]
    row = lax.broadcasted_iota(jnp.int32, (rows, count), 0)
    for part in range(2):
        pick = jnp.where(row == position + part * capacity, F32(1), F32(0)).astype(BF16)
        token_ref[:, part * half : (part + 1) * half] = dot(
            pick, rows_ref[:, :half], 0, 0
        ).astype(BF16)
        if part == 0:
            score = dot(rows_ref[:, half:], pick, 0, 0)
            grad_ref[...] = (score[0:1, :] / score_ref[...].astype(F32)).astype(BF16)


def combine(expert_ids, slot_index, gate_scores, rows, features, capacity):
    count = expert_ids.shape[0]
    return pl.pallas_call(
        functools.partial(combine_kernel, capacity),
        out_shape=[
            jax.ShapeDtypeStruct((count, features), BF16),
            jax.ShapeDtypeStruct((1, count), BF16),
        ],
        compiler_params=pltpu.CompilerParams(vmem_limit_bytes=24 * 2**20),
        name="combine",
    )(
        expert_ids.reshape(1, count),
        slot_index.reshape(1, count),
        gate_scores.reshape(1, count),
        rows,
    )


def halves_kernel(summed_hbm, sent_ref, kept_ref, sems):
    block = sent_ref.shape[0]
    copies = [
        pltpu.make_async_copy(summed_hbm.at[:block], sent_ref, sems.at[0]),
        pltpu.make_async_copy(summed_hbm.at[block:], kept_ref, sems.at[1]),
    ]
    for copy in copies:
        copy.start()
    for copy in copies:
        copy.wait()


def halves(summed):
    half = (summed.shape[0] // 2, summed.shape[1])
    return pl.pallas_call(
        halves_kernel,
        in_specs=[ANYWHERE],
        out_specs=[ON_CHIP, ON_CHIP],
        out_shape=[pltpu.VMEM(half, BF16), pltpu.VMEM(half, BF16)],
        scratch_shapes=[pltpu.SemaphoreType.DMA((2,))],
        name="halves",
    )(*in_hbm(summed))


def split_kernel(kept_ref, arrived_ref, gate_ref, up_ref, down_ref):
    hidden_size = gate_ref.shape[1]
    total = kept_ref[...].astype(F32) + arrived_ref[...].astype(F32)
    gate_ref[...] = total[:, :hidden_size].astype(BF16)
    up_ref[...] = total[:, hidden_size : 2 * hidden_size].astype(BF16)
    down_ref[...] = total[:, 2 * hidden_size :].T.astype(BF16)


def split_grads(kept, arrived):
    block, width = arrived.shape
    hidden_size = width // 3
    return pl.pallas_call(
        split_kernel,
        in_specs=[ON_CHIP, ON_CHIP],
        out_shape=[
            jax.ShapeDtypeStruct((block, hidden_size), BF16),
            jax.ShapeDtypeStruct((block, hidden_size), BF16),
            jax.ShapeDtypeStruct((hidden_size, block), BF16),
        ],
        name="split_grads",
    )(*on_chip(kept, arrived))


def on_device(
    tokens, cotangent, gate_scores, expert_ids, slot_index, gate_weight, up_weight, down_weight
):
    experts = lax.axis_size("expert")
    count, features = tokens.shape
    capacity = 2 * count // experts
    gate, up, down = gate_weight[0], up_weight[0], down_weight[0]
    send = dispatch(expert_ids, slot_index, gate_scores, tokens, cotangent, experts, capacity)
    received = lax.all_to_all(
        send.reshape(experts, 2 * capacity, features),
        "expert", split_axis=0, concat_axis=0, tiled=True,
    ).reshape(send.shape)
    ring = lax.axis_size("dp") // 2
    side = (lax.axis_index("dp") >= ring).astype(jnp.int32).reshape(1)
    grads, inner, score = expert_grads(side, ring, received, gate, up, down, capacity)
    summed = lax.psum_scatter(
        grads, "dp", scatter_dimension=0, tiled=True,
        axis_index_groups=[[s * ring + i for i in range(ring)] for s in range(2)],
    )
    back = return_rows(inner, score, gate, up, capacity)
    returned = lax.all_to_all(
        back.reshape(experts, 2 * capacity, back.shape[1]),
        "expert", split_axis=0, concat_axis=0, tiled=True,
    ).reshape(back.shape)
    summed, returned = lax.optimization_barrier((summed, returned))
    sent, kept = halves(summed)
    arrived = lax.ppermute(sent, "dp", [(i, (i + ring) % (2 * ring)) for i in range(2 * ring)])
    token_grad, score_grad = combine(
        expert_ids, slot_index, gate_scores, returned, features, capacity
    )
    grad_gate, grad_up, grad_down = split_grads(kept, arrived)
    return token_grad, score_grad.reshape(count), grad_gate[None], grad_up[None], grad_down[None]


def solution(mesh):
    both = ("expert", "dp")
    return jax.shard_map(
        on_device,
        mesh=mesh,
        in_specs=(
            P(both, None),
            P(both, None),
            P(both),
            P(both),
            P(both),
            P("expert", None, None),
            P("expert", None, None),
            P("expert", None, None),
        ),
        out_specs=(
            P(both, None),
            P(both),
            P("expert", "dp", None),
            P("expert", "dp", None),
            P("expert", None, "dp"),
        ),
        check_vma=False,
    )
```

```python
import functools

import jax
import jax.numpy as jnp
from jax import lax
from jax.experimental import pallas as pl
from jax.experimental.pallas import tpu as pltpu
from jax.sharding import PartitionSpec as P

F32 = jnp.float32
BF16 = jnp.bfloat16
LANES = 128


def dot(left, right, left_dim, right_dim):
    return lax.dot_general(
        left, right, (((left_dim,), (right_dim,)), ((), ())), preferred_element_type=F32
    )


def in_hbm(*arrays):
    return [pltpu.with_memory_space_constraint(array, pltpu.HBM) for array in arrays]


def on_chip(*arrays):
    return [pltpu.with_memory_space_constraint(array, pltpu.VMEM) for array in arrays]


ANYWHERE = pl.BlockSpec(memory_space=pltpu.HBM)
ON_CHIP = pl.BlockSpec(memory_space=pltpu.VMEM)
CHUNKS = 4


def dispatch_kernel(
    capacity, ids_hbm, slot_hbm, score_hbm, tokens_hbm, cotan_hbm, out_hbm,
    ids_ref, slot_ref, score_ref, rows_ref, out_ref, sems, out_sems,
):
    rows, (count, features) = out_ref.shape[0], tokens_hbm.shape
    chunk = features // CHUNKS
    columns = [slice(i * chunk, (i + 1) * chunk) for i in range(CHUNKS)]
    copies = [
        pltpu.make_async_copy(ids_hbm, ids_ref, sems.at[0]),
        pltpu.make_async_copy(slot_hbm, slot_ref, sems.at[1]),
        pltpu.make_async_copy(score_hbm, score_ref, sems.at[2]),
    ]
    for i, c in enumerate(columns):
        copies += [
            pltpu.make_async_copy(tokens_hbm.at[:, c], rows_ref.at[:count, c], sems.at[3 + 2 * i]),
            pltpu.make_async_copy(cotan_hbm.at[:, c], rows_ref.at[count:, c], sems.at[4 + 2 * i]),
        ]
    for copy in copies:
        copy.start()
    for copy in copies[:3]:
        copy.wait()
    position = ids_ref[...] * (2 * capacity) + slot_ref[...]
    row = lax.broadcasted_iota(jnp.int32, (rows, count), 0)
    pick_token = jnp.where(row == position, F32(1), F32(0))
    pick_cotan = jnp.where(row == position + capacity, score_ref[...].astype(F32), F32(0))
    pick = jnp.concatenate([pick_token, pick_cotan], axis=1).astype(BF16)
    writes = []
    for i, c in enumerate(columns):
        copies[3 + 2 * i].wait()
        copies[4 + 2 * i].wait()
        out_ref[:, c] = dot(pick, rows_ref[:, c], 1, 0).astype(BF16)
        writes.append(pltpu.make_async_copy(out_ref.at[:, c], out_hbm.at[:, c], out_sems.at[i]))
        writes[-1].start()
    for write in writes:
        write.wait()


def dispatch(expert_ids, slot_index, gate_scores, tokens, cotangent, experts, capacity):
    count, features = tokens.shape
    rows = experts * 2 * capacity
    return pl.pallas_call(
        functools.partial(dispatch_kernel, capacity),
        in_specs=[ANYWHERE] * 5,
        out_specs=ANYWHERE,
        out_shape=pltpu.HBM((rows, features), BF16),
        scratch_shapes=[
            pltpu.VMEM((1, count), jnp.int32),
            pltpu.VMEM((1, count), jnp.int32),
            pltpu.VMEM((1, count), BF16),
            pltpu.VMEM((2 * count, features), BF16),
            pltpu.VMEM((rows, features), BF16),
            pltpu.SemaphoreType.DMA((3 + 2 * CHUNKS,)),
            pltpu.SemaphoreType.DMA((CHUNKS,)),
        ],
        compiler_params=pltpu.CompilerParams(vmem_limit_bytes=24 * 2**20),
        name="dispatch",
    )(
        *in_hbm(
            expert_ids.reshape(1, count),
            slot_index.reshape(1, count),
            gate_scores.reshape(1, count),
            tokens,
            cotangent,
        )
    )


def pick_rows(slots, rows, capacity, half):
    slot = lax.broadcasted_iota(jnp.int32, (slots, rows), 0)
    row = lax.broadcasted_iota(jnp.int32, (slots, rows), 1)
    wanted = (slot // capacity) * (2 * capacity) + slot % capacity + half * capacity
    return jnp.where(row == wanted, F32(1), F32(0)).astype(BF16)


def expert_kernel(
    capacity, ring, place_ref, recv_ref, gate_hbm, up_hbm, down_hbm,
    gate_ref, up_ref, inner_ref, score_ref, *rest,
):
    grads, scratch = rest[: 2 * ring], rest[2 * ring :]
    down_ref, inputs, scaled, hidden_sc, stage, sems, out_sems = scratch
    rows, features = recv_ref.shape
    slots = rows // 2
    hidden_size = gate_ref.shape[1]
    side, spot = place_ref[0], place_ref[1]
    copies = [
        pltpu.make_async_copy(source, target, sems.at[i])
        for i, (source, target) in enumerate(
            ((gate_hbm, gate_ref), (up_hbm, up_ref), (down_hbm, down_ref))
        )
    ]
    for copy in copies:
        copy.start()
    received = recv_ref[...]
    inputs[...] = dot(pick_rows(slots, rows, capacity, 0), received, 1, 0).astype(BF16)
    scaled[...] = dot(pick_rows(slots, rows, capacity, 1), received, 1, 0).astype(BF16)
    copies[0].wait()
    pre_gate = dot(inputs[...], gate_ref[...], 1, 0)
    copies[1].wait()
    pre_up = dot(inputs[...], up_ref[...], 1, 0)
    copies[2].wait()
    hidden_grad = dot(scaled[...], down_ref[...], 1, 1)
    sigmoid = jax.nn.sigmoid(pre_gate)
    activated = pre_gate * sigmoid
    hidden = (activated * pre_up).astype(BF16)
    hidden_sc[...] = hidden
    inner_ref[:, :hidden_size] = (
        hidden_grad * pre_up * sigmoid * (1.0 + pre_gate * (1.0 - sigmoid))
    ).astype(BF16)
    inner_ref[:, hidden_size:] = (hidden_grad * activated).astype(BF16)
    score = jnp.sum(hidden.astype(F32) * hidden_grad, axis=1, keepdims=True)
    score_ref[...] = jnp.broadcast_to(score, score_ref.shape).astype(BF16)

    block = features // (2 * ring)
    writes = []
    for ahead in sorted(range(ring), key=lambda k: -min(k, ring - k)):
        for piece in range(2):
            owner = side if piece else 1 - side
            column = owner * ring + lax.rem(spot + ahead, ring)
            columns = pl.ds(pl.multiple_of(column * block, block), block)
            which = 2 * ahead + piece
            stage[which, :, : 2 * hidden_size] = dot(
                inputs[:, columns], inner_ref[...], 0, 0
            ).astype(BF16)
            stage[which, :, 2 * hidden_size :] = dot(
                scaled[:, columns], hidden_sc[...], 0, 0
            ).astype(BF16)
            writes.append(pltpu.make_async_copy(stage.at[which], grads[which], out_sems.at[which]))
            writes[-1].start()
    for write in writes:
        write.wait()


def expert_grads(place, ring, received, gate, up, down, capacity):
    rows, features = received.shape
    hidden_size = gate.shape[1]
    slots = rows // 2
    block = (features // (2 * ring), 3 * hidden_size)
    return pl.pallas_call(
        functools.partial(expert_kernel, capacity, ring),
        in_specs=[pl.BlockSpec(memory_space=pltpu.SMEM), ON_CHIP, ANYWHERE, ANYWHERE, ANYWHERE],
        out_specs=[ON_CHIP] * 4 + [ANYWHERE] * (2 * ring),
        out_shape=[
            pltpu.VMEM(gate.shape, BF16),
            pltpu.VMEM(up.shape, BF16),
            pltpu.VMEM((slots, 2 * hidden_size), BF16),
            pltpu.VMEM((slots, LANES), BF16),
        ]
        + [pltpu.HBM(block, BF16)] * (2 * ring),
        scratch_shapes=[
            pltpu.VMEM(down.shape, BF16),
            pltpu.VMEM((slots, features), BF16),
            pltpu.VMEM((slots, features), BF16),
            pltpu.VMEM((slots, hidden_size), BF16),
            pltpu.VMEM((2 * ring, *block), BF16),
            pltpu.SemaphoreType.DMA((3,)),
            pltpu.SemaphoreType.DMA((2 * ring,)),
        ],
        compiler_params=pltpu.CompilerParams(vmem_limit_bytes=28 * 2**20),
        name="expert_grads",
    )(place, *on_chip(received), *in_hbm(gate, up, down))


def return_kernel(capacity, inner_ref, score_ref, gate_ref, up_ref, out_ref):
    slots = inner_ref.shape[0]
    rows = out_ref.shape[0]
    hidden_size = gate_ref.shape[1]
    half = gate_ref.shape[0] // 2
    total = jnp.zeros((rows, half), F32)
    for part in range(2):
        piece = pl.ds(part * half, half)
        input_grad = dot(inner_ref[:, :hidden_size], gate_ref[piece, :], 1, 1) + dot(
            inner_ref[:, hidden_size:], up_ref[piece, :], 1, 1
        )
        spread = pick_rows(slots, rows, capacity, part)
        total += dot(spread, input_grad.astype(BF16), 0, 0)
        if part == 0:
            out_ref[:, half:] = dot(spread, score_ref[...], 0, 0).astype(BF16)
    out_ref[:, :half] = total.astype(BF16)


def return_rows(inner, score, gate, up, capacity):
    slots = inner.shape[0]
    half = gate.shape[0] // 2
    return pl.pallas_call(
        functools.partial(return_kernel, capacity),
        out_shape=jax.ShapeDtypeStruct((2 * slots, half + LANES), BF16),
        compiler_params=pltpu.CompilerParams(vmem_limit_bytes=24 * 2**20),
        name="return_rows",
    )(*on_chip(inner, score, gate, up))


def combine_kernel(capacity, ids_ref, slot_ref, score_ref, rows_ref, token_ref, grad_ref):
    rows = rows_ref.shape[0]
    count = token_ref.shape[0]
    half = token_ref.shape[1] // 2
    position = ids_ref[...] * (2 * capacity) + slot_ref[...]
    row = lax.broadcasted_iota(jnp.int32, (rows, count), 0)
    for part in range(2):
        pick = jnp.where(row == position + part * capacity, F32(1), F32(0)).astype(BF16)
        token_ref[:, part * half : (part + 1) * half] = dot(
            pick, rows_ref[:, :half], 0, 0
        ).astype(BF16)
        if part == 0:
            score = dot(rows_ref[:, half:], pick, 0, 0)
            grad_ref[...] = (score[0:1, :] / score_ref[...].astype(F32)).astype(BF16)


def combine(expert_ids, slot_index, gate_scores, rows, features, capacity):
    count = expert_ids.shape[0]
    return pl.pallas_call(
        functools.partial(combine_kernel, capacity),
        out_shape=[
            jax.ShapeDtypeStruct((count, features), BF16),
            jax.ShapeDtypeStruct((1, count), BF16),
        ],
        compiler_params=pltpu.CompilerParams(vmem_limit_bytes=24 * 2**20),
        name="combine",
    )(
        *in_hbm(
            expert_ids.reshape(1, count),
            slot_index.reshape(1, count),
            gate_scores.reshape(1, count),
        ),
        *on_chip(rows),
    )


def add_kernel(*refs):
    total = refs[0][...].astype(F32)
    for ref in refs[1:-1]:
        total += ref[...].astype(F32)
    refs[-1][...] = total.astype(BF16)


def add(*arrays):
    return pl.pallas_call(
        add_kernel,
        in_specs=[ON_CHIP] * len(arrays),
        out_specs=ON_CHIP,
        out_shape=pltpu.VMEM(arrays[0].shape, BF16),
        compiler_params=pltpu.CompilerParams(vmem_limit_bytes=6 * 2**20),
        name="add",
    )(*on_chip(*arrays))


def split_kernel(own_ref, up_way_ref, down_way_ref, other_ref, gate_ref, up_ref, down_ref):
    hidden_size = gate_ref.shape[1]
    total = own_ref[...].astype(F32) + up_way_ref[...].astype(F32)
    total += down_way_ref[...].astype(F32) + other_ref[...].astype(F32)
    gate_ref[...] = total[:, :hidden_size].astype(BF16)
    up_ref[...] = total[:, hidden_size : 2 * hidden_size].astype(BF16)
    down_ref[...] = total[:, 2 * hidden_size :].T.astype(BF16)


def split_grads(*parts):
    block, width = parts[0].shape
    hidden_size = width // 3
    return pl.pallas_call(
        split_kernel,
        in_specs=[ON_CHIP] * 4,
        out_shape=[
            jax.ShapeDtypeStruct((block, hidden_size), BF16),
            jax.ShapeDtypeStruct((block, hidden_size), BF16),
            jax.ShapeDtypeStruct((hidden_size, block), BF16),
        ],
        name="split_grads",
    )(*on_chip(*parts))


def ring_sums(grads, ring):
    far = ring // 2
    moves = {
        way: [(s * ring + i, s * ring + (i + way) % ring) for s in range(2) for i in range(ring)]
        for way in (1, -1)
    }
    block = lambda ahead, piece: grads[2 * (ahead % ring) + piece]
    carried = {}
    for hop in range(far, 0, -1):
        for piece in range(2):
            for way in (1, -1):
                if hop == far and piece != (0 if way == 1 else 1):
                    continue
                own = block(way * hop, piece)
                if (way, piece) in carried:
                    own = add(own, carried[way, piece])
                carried[way, piece] = lax.ppermute(own, "dp", moves[way])
    return [
        (block(0, piece), carried[1, piece], carried[-1, piece]) for piece in range(2)
    ]


def on_device(
    tokens, cotangent, gate_scores, expert_ids, slot_index, gate_weight, up_weight, down_weight
):
    experts = lax.axis_size("expert")
    count, features = tokens.shape
    capacity = 2 * count // experts
    gate, up, down = gate_weight[0], up_weight[0], down_weight[0]
    send = dispatch(expert_ids, slot_index, gate_scores, tokens, cotangent, experts, capacity)
    received = lax.all_to_all(
        send.reshape(experts, 2 * capacity, features),
        "expert", split_axis=0, concat_axis=0, tiled=True,
    ).reshape(send.shape)
    ring = lax.axis_size("dp") // 2
    index = lax.axis_index("dp")
    side = (index >= ring).astype(jnp.int32)
    place = jnp.stack([side, index - side * ring])
    gate, up, inner, score, *grads = expert_grads(place, ring, received, gate, up, down, capacity)
    back = return_rows(inner, score, gate, up, capacity)
    returned = lax.all_to_all(
        back.reshape(experts, 2 * capacity, back.shape[1]),
        "expert", split_axis=0, concat_axis=0, tiled=True,
    ).reshape(back.shape)
    for_other, kept = ring_sums(grads, ring)
    other = lax.ppermute(
        add(*for_other), "dp", [(i, (i + ring) % (2 * ring)) for i in range(2 * ring)]
    )
    token_grad, score_grad = combine(
        expert_ids, slot_index, gate_scores, returned, features, capacity
    )
    grad_gate, grad_up, grad_down = split_grads(*kept, other)
    return token_grad, score_grad.reshape(count), grad_gate[None], grad_up[None], grad_down[None]


def solution(mesh):
    both = ("expert", "dp")
    return jax.shard_map(
        on_device,
        mesh=mesh,
        in_specs=(
            P(both, None),
            P(both, None),
            P(both),
            P(both),
            P(both),
            P("expert", None, None),
            P("expert", None, None),
            P("expert", None, None),
        ),
        out_specs=(
            P(both, None),
            P(both),
            P("expert", "dp", None),
            P("expert", "dp", None),
            P("expert", None, "dp"),
        ),
        check_vma=False,
    )
```

```python
import functools

import jax
import jax.numpy as jnp
from jax import lax
from jax.experimental import pallas as pl
from jax.experimental.pallas import tpu as pltpu
from jax.sharding import PartitionSpec as P

F32 = jnp.float32
BF16 = jnp.bfloat16
LANES = 128


def dot(left, right, left_dim, right_dim):
    return lax.dot_general(
        left, right, (((left_dim,), (right_dim,)), ((), ())), preferred_element_type=F32
    )


def in_hbm(*arrays):
    return [pltpu.with_memory_space_constraint(array, pltpu.HBM) for array in arrays]


def on_chip(*arrays):
    return [pltpu.with_memory_space_constraint(array, pltpu.VMEM) for array in arrays]


ANYWHERE = pl.BlockSpec(memory_space=pltpu.HBM)
ON_CHIP = pl.BlockSpec(memory_space=pltpu.VMEM)
CHUNKS = 4


def dispatch_kernel(
    capacity, ids_hbm, slot_hbm, score_hbm, tokens_hbm, cotan_hbm, out_hbm,
    ids_ref, slot_ref, score_ref, rows_ref, out_ref, sems, out_sems,
):
    rows, (count, features) = out_ref.shape[0], tokens_hbm.shape
    chunk = features // CHUNKS
    columns = [slice(i * chunk, (i + 1) * chunk) for i in range(CHUNKS)]
    copies = [
        pltpu.make_async_copy(ids_hbm, ids_ref, sems.at[0]),
        pltpu.make_async_copy(slot_hbm, slot_ref, sems.at[1]),
        pltpu.make_async_copy(score_hbm, score_ref, sems.at[2]),
    ]
    for i, c in enumerate(columns):
        copies += [
            pltpu.make_async_copy(tokens_hbm.at[:, c], rows_ref.at[:count, c], sems.at[3 + 2 * i]),
            pltpu.make_async_copy(cotan_hbm.at[:, c], rows_ref.at[count:, c], sems.at[4 + 2 * i]),
        ]
    for copy in copies:
        copy.start()
    for copy in copies[:3]:
        copy.wait()
    position = ids_ref[...] * (2 * capacity) + slot_ref[...]
    row = lax.broadcasted_iota(jnp.int32, (rows, count), 0)
    pick_token = jnp.where(row == position, F32(1), F32(0))
    pick_cotan = jnp.where(row == position + capacity, score_ref[...].astype(F32), F32(0))
    pick = jnp.concatenate([pick_token, pick_cotan], axis=1).astype(BF16)
    writes = []
    for i, c in enumerate(columns):
        copies[3 + 2 * i].wait()
        copies[4 + 2 * i].wait()
        out_ref[:, c] = dot(pick, rows_ref[:, c], 1, 0).astype(BF16)
        writes.append(pltpu.make_async_copy(out_ref.at[:, c], out_hbm.at[:, c], out_sems.at[i]))
        writes[-1].start()
    for write in writes:
        write.wait()


def dispatch(expert_ids, slot_index, gate_scores, tokens, cotangent, experts, capacity):
    count, features = tokens.shape
    rows = experts * 2 * capacity
    return pl.pallas_call(
        functools.partial(dispatch_kernel, capacity),
        in_specs=[ANYWHERE] * 5,
        out_specs=ANYWHERE,
        out_shape=pltpu.HBM((rows, features), BF16),
        scratch_shapes=[
            pltpu.VMEM((1, count), jnp.int32),
            pltpu.VMEM((1, count), jnp.int32),
            pltpu.VMEM((1, count), BF16),
            pltpu.VMEM((2 * count, features), BF16),
            pltpu.VMEM((rows, features), BF16),
            pltpu.SemaphoreType.DMA((3 + 2 * CHUNKS,)),
            pltpu.SemaphoreType.DMA((CHUNKS,)),
        ],
        compiler_params=pltpu.CompilerParams(vmem_limit_bytes=24 * 2**20),
        name="dispatch",
    )(
        *in_hbm(
            expert_ids.reshape(1, count),
            slot_index.reshape(1, count),
            gate_scores.reshape(1, count),
            tokens,
            cotangent,
        )
    )


def pick_rows(slots, rows, capacity, half):
    slot = lax.broadcasted_iota(jnp.int32, (slots, rows), 0)
    row = lax.broadcasted_iota(jnp.int32, (slots, rows), 1)
    wanted = (slot // capacity) * (2 * capacity) + slot % capacity + half * capacity
    return jnp.where(row == wanted, F32(1), F32(0)).astype(BF16)


def early_blocks(ring):
    return [(ring // 2, 0), (2, 0), (ring - 2, 0)]


def late_blocks(ring):
    far = sorted(range(ring), key=lambda k: -min(k, ring - k))
    return [(k, p) for k in far for p in range(2) if (k, p) not in early_blocks(ring)]


def write_blocks(blocks, ring, place_ref, inputs, scaled, inner, hidden, stage, outs, sems):
    side, spot = place_ref[0], place_ref[1]
    block = inputs.shape[1] // (2 * ring)
    hidden_size = hidden.shape[1]
    writes = []
    for i, (ahead, piece) in enumerate(blocks):
        owner = side if piece else 1 - side
        column = owner * ring + lax.rem(spot + ahead, ring)
        columns = pl.ds(pl.multiple_of(column * block, block), block)
        stage[i, :, : 2 * hidden_size] = dot(inputs[:, columns], inner[...], 0, 0).astype(BF16)
        stage[i, :, 2 * hidden_size :] = dot(scaled[:, columns], hidden[...], 0, 0).astype(BF16)
        writes.append(pltpu.make_async_copy(stage.at[i], outs[i], sems.at[i]))
        writes[-1].start()
    return writes


def expert_kernel(
    capacity, ring, place_ref, recv_ref, gate_hbm, up_hbm, down_hbm,
    gate_ref, up_ref, inner_ref, score_ref, inputs, scaled, hidden_ref, *rest,
):
    blocks = early_blocks(ring)
    grads, (down_ref, stage, sems, out_sems) = rest[: len(blocks)], rest[len(blocks) :]
    rows, features = recv_ref.shape
    slots = rows // 2
    hidden_size = gate_ref.shape[1]
    copies = [
        pltpu.make_async_copy(source, target, sems.at[i])
        for i, (source, target) in enumerate(
            ((gate_hbm, gate_ref), (up_hbm, up_ref), (down_hbm, down_ref))
        )
    ]
    for copy in copies:
        copy.start()
    received = recv_ref[...]
    inputs[...] = dot(pick_rows(slots, rows, capacity, 0), received, 1, 0).astype(BF16)
    scaled[...] = dot(pick_rows(slots, rows, capacity, 1), received, 1, 0).astype(BF16)
    copies[0].wait()
    pre_gate = dot(inputs[...], gate_ref[...], 1, 0)
    copies[1].wait()
    pre_up = dot(inputs[...], up_ref[...], 1, 0)
    copies[2].wait()
    hidden_grad = dot(scaled[...], down_ref[...], 1, 1)
    sigmoid = jax.nn.sigmoid(pre_gate)
    activated = pre_gate * sigmoid
    hidden = (activated * pre_up).astype(BF16)
    hidden_ref[...] = hidden
    inner_ref[:, :hidden_size] = (
        hidden_grad * pre_up * sigmoid * (1.0 + pre_gate * (1.0 - sigmoid))
    ).astype(BF16)
    inner_ref[:, hidden_size:] = (hidden_grad * activated).astype(BF16)
    score = jnp.sum(hidden.astype(F32) * hidden_grad, axis=1, keepdims=True)
    score_ref[...] = jnp.broadcast_to(score, score_ref.shape).astype(BF16)
    for write in write_blocks(
        blocks, ring, place_ref, inputs, scaled, inner_ref, hidden_ref, stage, grads, out_sems
    ):
        write.wait()


def expert_first(place, ring, received, gate, up, down, capacity):
    rows, features = received.shape
    hidden_size = gate.shape[1]
    slots = rows // 2
    block = (features // (2 * ring), 3 * hidden_size)
    count = len(early_blocks(ring))
    return pl.pallas_call(
        functools.partial(expert_kernel, capacity, ring),
        in_specs=[pl.BlockSpec(memory_space=pltpu.SMEM), ON_CHIP, ANYWHERE, ANYWHERE, ANYWHERE],
        out_specs=[ON_CHIP] * 7 + [ANYWHERE] * count,
        out_shape=[
            pltpu.VMEM(gate.shape, BF16),
            pltpu.VMEM(up.shape, BF16),
            pltpu.VMEM((slots, 2 * hidden_size), BF16),
            pltpu.VMEM((slots, LANES), BF16),
            pltpu.VMEM((slots, features), BF16),
            pltpu.VMEM((slots, features), BF16),
            pltpu.VMEM((slots, hidden_size), BF16),
        ]
        + [pltpu.HBM(block, BF16)] * count,
        scratch_shapes=[
            pltpu.VMEM(down.shape, BF16),
            pltpu.VMEM((count, *block), BF16),
            pltpu.SemaphoreType.DMA((3,)),
            pltpu.SemaphoreType.DMA((count,)),
        ],
        compiler_params=pltpu.CompilerParams(vmem_limit_bytes=24 * 2**20),
        name="expert_first",
    )(place, *on_chip(received), *in_hbm(gate, up, down))


def late_kernel(
    capacity, ring, place_ref, gate_ref, up_ref, inner_ref, score_ref, inputs, scaled, hidden_ref,
    back_hbm, *rest,
):
    blocks = late_blocks(ring)
    grads, (stage, back, out_sems) = rest[: len(blocks)], rest[len(blocks) :]
    slots = inner_ref.shape[0]
    rows = back.shape[0]
    hidden_size = gate_ref.shape[1]
    half = gate_ref.shape[0] // 2
    writes = write_blocks(
        blocks, ring, place_ref, inputs, scaled, inner_ref, hidden_ref, stage, grads, out_sems
    )
    total = jnp.zeros((rows, half), F32)
    for part in range(2):
        piece = pl.ds(part * half, half)
        input_grad = dot(inner_ref[:, :hidden_size], gate_ref[piece, :], 1, 1) + dot(
            inner_ref[:, hidden_size:], up_ref[piece, :], 1, 1
        )
        spread = pick_rows(slots, rows, capacity, part)
        total += dot(spread, input_grad.astype(BF16), 0, 0)
        if part == 0:
            back[:, half:] = dot(spread, score_ref[...], 0, 0).astype(BF16)
    back[:, :half] = total.astype(BF16)
    writes.append(pltpu.make_async_copy(back, back_hbm, out_sems.at[len(blocks)]))
    writes[-1].start()
    for write in writes:
        write.wait()


def expert_late(place, ring, gate, up, inner, score, inputs, scaled, hidden, capacity):
    slots, features = inputs.shape
    hidden_size = gate.shape[1]
    block = (features // (2 * ring), 3 * hidden_size)
    count = len(late_blocks(ring))
    back = (2 * slots, features // 2 + LANES)
    return pl.pallas_call(
        functools.partial(late_kernel, capacity, ring),
        in_specs=[pl.BlockSpec(memory_space=pltpu.SMEM)] + [ON_CHIP] * 7,
        out_specs=[ANYWHERE] * (1 + count),
        out_shape=[pltpu.HBM(back, BF16)] + [pltpu.HBM(block, BF16)] * count,
        scratch_shapes=[
            pltpu.VMEM((count, *block), BF16),
            pltpu.VMEM(back, BF16),
            pltpu.SemaphoreType.DMA((count + 1,)),
        ],
        compiler_params=pltpu.CompilerParams(vmem_limit_bytes=24 * 2**20),
        cost_estimate=pl.CostEstimate(
            flops=2 * slots * features * 6 * hidden_size, bytes_accessed=2**23, transcendentals=0
        ),
        name="expert_late",
    )(place, *on_chip(gate, up, inner, score, inputs, scaled, hidden))


def combine_kernel(capacity, ids_ref, slot_ref, score_ref, rows_ref, token_ref, grad_ref):
    rows = rows_ref.shape[0]
    count = token_ref.shape[0]
    half = token_ref.shape[1] // 2
    position = ids_ref[...] * (2 * capacity) + slot_ref[...]
    row = lax.broadcasted_iota(jnp.int32, (rows, count), 0)
    for part in range(2):
        pick = jnp.where(row == position + part * capacity, F32(1), F32(0)).astype(BF16)
        token_ref[:, part * half : (part + 1) * half] = dot(
            pick, rows_ref[:, :half], 0, 0
        ).astype(BF16)
        if part == 0:
            score = dot(rows_ref[:, half:], pick, 0, 0)
            grad_ref[...] = (score[0:1, :] / score_ref[...].astype(F32)).astype(BF16)


def combine(expert_ids, slot_index, gate_scores, rows, features, capacity):
    count = expert_ids.shape[0]
    return pl.pallas_call(
        functools.partial(combine_kernel, capacity),
        out_shape=[
            jax.ShapeDtypeStruct((count, features), BF16),
            jax.ShapeDtypeStruct((1, count), BF16),
        ],
        compiler_params=pltpu.CompilerParams(vmem_limit_bytes=24 * 2**20),
        name="combine",
    )(
        *in_hbm(
            expert_ids.reshape(1, count),
            slot_index.reshape(1, count),
            gate_scores.reshape(1, count),
        ),
        *on_chip(rows),
    )


def add_kernel(*refs):
    total = refs[0][...].astype(F32)
    for ref in refs[1:-1]:
        total += ref[...].astype(F32)
    refs[-1][...] = total.astype(BF16)


def add(*arrays):
    return pl.pallas_call(
        add_kernel,
        in_specs=[ON_CHIP] * len(arrays),
        out_specs=ON_CHIP,
        out_shape=pltpu.VMEM(arrays[0].shape, BF16),
        compiler_params=pltpu.CompilerParams(vmem_limit_bytes=6 * 2**20),
        name="add",
    )(*on_chip(*arrays))


def split_kernel(own_ref, up_way_ref, down_way_ref, other_ref, gate_ref, up_ref, down_ref):
    hidden_size = gate_ref.shape[1]
    total = own_ref[...].astype(F32) + up_way_ref[...].astype(F32)
    total += down_way_ref[...].astype(F32) + other_ref[...].astype(F32)
    gate_ref[...] = total[:, :hidden_size].astype(BF16)
    up_ref[...] = total[:, hidden_size : 2 * hidden_size].astype(BF16)
    down_ref[...] = total[:, 2 * hidden_size :].T.astype(BF16)


def split_grads(*parts):
    block, width = parts[0].shape
    hidden_size = width // 3
    return pl.pallas_call(
        split_kernel,
        in_specs=[ON_CHIP] * 4,
        out_shape=[
            jax.ShapeDtypeStruct((block, hidden_size), BF16),
            jax.ShapeDtypeStruct((block, hidden_size), BF16),
            jax.ShapeDtypeStruct((hidden_size, block), BF16),
        ],
        name="split_grads",
    )(*on_chip(*parts))


def ring_sums(grads, ring):
    far = ring // 2
    moves = {
        way: [(s * ring + i, s * ring + (i + way) % ring) for s in range(2) for i in range(ring)]
        for way in (1, -1)
    }
    across = lambda block: lax.ppermute(
        block, "dp", [(i, (i + ring) % (2 * ring)) for i in range(2 * ring)]
    )
    block = lambda ahead, piece: grads[ahead % ring, piece]
    joined = {k % ring: add(block(k, 1), across(block(k, 0))) for k in (far, far - 1, 1 - far)}
    carried = {}
    for hop in range(far, 0, -1):
        for piece in range(2):
            for way in (1, -1):
                if piece == 0 and hop > 2 or hop == far and way == -1:
                    continue
                own = block(way * hop, piece)
                if piece == 1:
                    own = joined.get(way * hop % ring, own)
                if (way, piece) in carried:
                    own = add(own, carried[way, piece])
                carried[way, piece] = lax.ppermute(own, "dp", moves[way])
    other = across(add(block(0, 0), carried[1, 0], carried[-1, 0]))
    return block(0, 1), carried[1, 1], carried[-1, 1], other


def on_device(
    tokens, cotangent, gate_scores, expert_ids, slot_index, gate_weight, up_weight, down_weight
):
    experts = lax.axis_size("expert")
    count, features = tokens.shape
    capacity = 2 * count // experts
    gate, up, down = gate_weight[0], up_weight[0], down_weight[0]
    send = dispatch(expert_ids, slot_index, gate_scores, tokens, cotangent, experts, capacity)
    received = lax.all_to_all(
        send.reshape(experts, 2 * capacity, features),
        "expert", split_axis=0, concat_axis=0, tiled=True,
    ).reshape(send.shape)
    ring = lax.axis_size("dp") // 2
    index = lax.axis_index("dp")
    side = (index >= ring).astype(jnp.int32)
    place = jnp.stack([side, index - side * ring])
    held = expert_first(place, ring, received, gate, up, down, capacity)
    held, early = held[:7], held[7:]
    back, *late = expert_late(place, ring, *held, capacity)
    grads = dict(zip(early_blocks(ring) + late_blocks(ring), [*early, *late]))
    returned = lax.all_to_all(
        back.reshape(experts, 2 * capacity, back.shape[1]),
        "expert", split_axis=0, concat_axis=0, tiled=True,
    ).reshape(back.shape)
    *parts, other = ring_sums(grads, ring)
    token_grad, score_grad = combine(
        expert_ids, slot_index, gate_scores, returned, features, capacity
    )
    other, score_grad = lax.optimization_barrier((other, score_grad))
    grad_gate, grad_up, grad_down = split_grads(*parts, other)
    return token_grad, score_grad.reshape(count), grad_gate[None], grad_up[None], grad_down[None]


def solution(mesh):
    both = ("expert", "dp")
    return jax.shard_map(
        on_device,
        mesh=mesh,
        in_specs=(
            P(both, None),
            P(both, None),
            P(both),
            P(both),
            P(both),
            P("expert", None, None),
            P("expert", None, None),
            P("expert", None, None),
        ),
        out_specs=(
            P(both, None),
            P(both),
            P("expert", "dp", None),
            P("expert", "dp", None),
            P("expert", None, "dp"),
        ),
        check_vma=False,
    )
```

```python
import functools

import jax
import jax.numpy as jnp
from jax import lax
from jax.experimental import pallas as pl
from jax.experimental.pallas import tpu as pltpu
from jax.sharding import PartitionSpec as P

F32 = jnp.float32
BF16 = jnp.bfloat16
LANES = 128


def dot(left, right, left_dim, right_dim):
    return lax.dot_general(
        left, right, (((left_dim,), (right_dim,)), ((), ())), preferred_element_type=F32
    )


def in_hbm(*arrays):
    return [pltpu.with_memory_space_constraint(array, pltpu.HBM) for array in arrays]


def on_chip(*arrays):
    return [pltpu.with_memory_space_constraint(array, pltpu.VMEM) for array in arrays]


ANYWHERE = pl.BlockSpec(memory_space=pltpu.HBM)
ON_CHIP = pl.BlockSpec(memory_space=pltpu.VMEM)
CHUNKS = 4


def dispatch_kernel(
    capacity, ids_hbm, slot_hbm, score_hbm, tokens_hbm, cotan_hbm, out_hbm,
    ids_ref, slot_ref, score_ref, rows_ref, out_ref, sems, out_sems,
):
    rows, (count, features) = out_ref.shape[0], tokens_hbm.shape
    chunk = features // CHUNKS
    columns = [slice(i * chunk, (i + 1) * chunk) for i in range(CHUNKS)]
    copies = [
        pltpu.make_async_copy(ids_hbm, ids_ref, sems.at[0]),
        pltpu.make_async_copy(slot_hbm, slot_ref, sems.at[1]),
        pltpu.make_async_copy(score_hbm, score_ref, sems.at[2]),
    ]
    for i, c in enumerate(columns):
        copies += [
            pltpu.make_async_copy(tokens_hbm.at[:, c], rows_ref.at[:count, c], sems.at[3 + 2 * i]),
            pltpu.make_async_copy(cotan_hbm.at[:, c], rows_ref.at[count:, c], sems.at[4 + 2 * i]),
        ]
    for copy in copies:
        copy.start()
    for copy in copies[:3]:
        copy.wait()
    position = ids_ref[...] * (2 * capacity) + slot_ref[...]
    row = lax.broadcasted_iota(jnp.int32, (rows, count), 0)
    pick_token = jnp.where(row == position, F32(1), F32(0))
    pick_cotan = jnp.where(row == position + capacity, score_ref[...].astype(F32), F32(0))
    pick = jnp.concatenate([pick_token, pick_cotan], axis=1).astype(BF16)
    writes = []
    for i, c in enumerate(columns):
        copies[3 + 2 * i].wait()
        copies[4 + 2 * i].wait()
        out_ref[:, c] = dot(pick, rows_ref[:, c], 1, 0).astype(BF16)
        writes.append(pltpu.make_async_copy(out_ref.at[:, c], out_hbm.at[:, c], out_sems.at[i]))
        writes[-1].start()
    for write in writes:
        write.wait()


def dispatch(expert_ids, slot_index, gate_scores, tokens, cotangent, experts, capacity):
    count, features = tokens.shape
    rows = experts * 2 * capacity
    return pl.pallas_call(
        functools.partial(dispatch_kernel, capacity),
        in_specs=[ANYWHERE] * 5,
        out_specs=ANYWHERE,
        out_shape=pltpu.HBM((rows, features), BF16),
        scratch_shapes=[
            pltpu.VMEM((1, count), jnp.int32),
            pltpu.VMEM((1, count), jnp.int32),
            pltpu.VMEM((1, count), BF16),
            pltpu.VMEM((2 * count, features), BF16),
            pltpu.VMEM((rows, features), BF16),
            pltpu.SemaphoreType.DMA((3 + 2 * CHUNKS,)),
            pltpu.SemaphoreType.DMA((CHUNKS,)),
        ],
        compiler_params=pltpu.CompilerParams(vmem_limit_bytes=24 * 2**20),
        name="dispatch",
    )(
        *in_hbm(
            expert_ids.reshape(1, count),
            slot_index.reshape(1, count),
            gate_scores.reshape(1, count),
            tokens,
            cotangent,
        )
    )


def pick_rows(slots, rows, capacity, half):
    slot = lax.broadcasted_iota(jnp.int32, (slots, rows), 0)
    row = lax.broadcasted_iota(jnp.int32, (slots, rows), 1)
    wanted = (slot // capacity) * (2 * capacity) + slot % capacity + half * capacity
    return jnp.where(row == wanted, F32(1), F32(0)).astype(BF16)


def early_blocks(ring):
    far = ring // 2
    return [(far, 0), (far, 1), (far - 1, 1), (far + 1, 0)]


def late_blocks(ring):
    far = sorted(range(ring), key=lambda k: -min(k, ring - k))
    return [(k, p) for k in far for p in range(2) if (k, p) not in early_blocks(ring)]


def write_blocks(blocks, ring, place_ref, inputs, scaled, inner, hidden, stage, outs, sems):
    side, spot = place_ref[0], place_ref[1]
    block = inputs.shape[1] // (2 * ring)
    hidden_size = hidden.shape[1]
    writes = []
    for i, (ahead, piece) in enumerate(blocks):
        owner = side if piece else 1 - side
        column = owner * ring + lax.rem(spot + ahead, ring)
        columns = pl.ds(pl.multiple_of(column * block, block), block)
        stage[i, :, : 2 * hidden_size] = dot(inputs[:, columns], inner[...], 0, 0).astype(BF16)
        stage[i, :, 2 * hidden_size :] = dot(scaled[:, columns], hidden[...], 0, 0).astype(BF16)
        writes.append(pltpu.make_async_copy(stage.at[i], outs[i], sems.at[i]))
        writes[-1].start()
    return writes


def expert_kernel(
    capacity, ring, place_ref, recv_ref, gate_hbm, up_hbm, down_hbm,
    gate_ref, up_ref, inner_ref, score_ref, inputs, scaled, hidden_ref, *rest,
):
    blocks = early_blocks(ring)
    grads, (down_ref, stage, sems, out_sems) = rest[: len(blocks)], rest[len(blocks) :]
    rows, features = recv_ref.shape
    slots = rows // 2
    hidden_size = gate_ref.shape[1]
    copies = [
        pltpu.make_async_copy(source, target, sems.at[i])
        for i, (source, target) in enumerate(
            ((gate_hbm, gate_ref), (up_hbm, up_ref), (down_hbm, down_ref))
        )
    ]
    for copy in copies:
        copy.start()
    received = recv_ref[...]
    inputs[...] = dot(pick_rows(slots, rows, capacity, 0), received, 1, 0).astype(BF16)
    scaled[...] = dot(pick_rows(slots, rows, capacity, 1), received, 1, 0).astype(BF16)
    copies[0].wait()
    pre_gate = dot(inputs[...], gate_ref[...], 1, 0)
    copies[1].wait()
    pre_up = dot(inputs[...], up_ref[...], 1, 0)
    copies[2].wait()
    hidden_grad = dot(scaled[...], down_ref[...], 1, 1)
    sigmoid = jax.nn.sigmoid(pre_gate)
    activated = pre_gate * sigmoid
    hidden = (activated * pre_up).astype(BF16)
    hidden_ref[...] = hidden
    inner_ref[:, :hidden_size] = (
        hidden_grad * pre_up * sigmoid * (1.0 + pre_gate * (1.0 - sigmoid))
    ).astype(BF16)
    inner_ref[:, hidden_size:] = (hidden_grad * activated).astype(BF16)
    score = jnp.sum(hidden.astype(F32) * hidden_grad, axis=1, keepdims=True)
    score_ref[...] = jnp.broadcast_to(score, score_ref.shape).astype(BF16)
    for write in write_blocks(
        blocks, ring, place_ref, inputs, scaled, inner_ref, hidden_ref, stage, grads, out_sems
    ):
        write.wait()


def expert_first(place, ring, received, gate, up, down, capacity):
    rows, features = received.shape
    hidden_size = gate.shape[1]
    slots = rows // 2
    block = (features // (2 * ring), 3 * hidden_size)
    count = len(early_blocks(ring))
    return pl.pallas_call(
        functools.partial(expert_kernel, capacity, ring),
        in_specs=[pl.BlockSpec(memory_space=pltpu.SMEM), ON_CHIP, ANYWHERE, ANYWHERE, ANYWHERE],
        out_specs=[ON_CHIP] * 7 + [ANYWHERE] * count,
        out_shape=[
            pltpu.VMEM(gate.shape, BF16),
            pltpu.VMEM(up.shape, BF16),
            pltpu.VMEM((slots, 2 * hidden_size), BF16),
            pltpu.VMEM((slots, LANES), BF16),
            pltpu.VMEM((slots, features), BF16),
            pltpu.VMEM((slots, features), BF16),
            pltpu.VMEM((slots, hidden_size), BF16),
        ]
        + [pltpu.HBM(block, BF16)] * count,
        scratch_shapes=[
            pltpu.VMEM(down.shape, BF16),
            pltpu.VMEM((count, *block), BF16),
            pltpu.SemaphoreType.DMA((3,)),
            pltpu.SemaphoreType.DMA((count,)),
        ],
        compiler_params=pltpu.CompilerParams(vmem_limit_bytes=24 * 2**20),
        name="expert_first",
    )(place, *on_chip(received), *in_hbm(gate, up, down))


def late_kernel(
    capacity, ring, place_ref, gate_ref, up_ref, inner_ref, score_ref, inputs, scaled, hidden_ref,
    back_hbm, *rest,
):
    blocks = late_blocks(ring)
    grads, (stage, back, out_sems) = rest[: len(blocks)], rest[len(blocks) :]
    slots = inner_ref.shape[0]
    rows = back.shape[0]
    hidden_size = gate_ref.shape[1]
    half = gate_ref.shape[0] // 2
    writes = write_blocks(
        blocks, ring, place_ref, inputs, scaled, inner_ref, hidden_ref, stage, grads, out_sems
    )
    total = jnp.zeros((rows, half), F32)
    for part in range(2):
        piece = pl.ds(part * half, half)
        input_grad = dot(inner_ref[:, :hidden_size], gate_ref[piece, :], 1, 1) + dot(
            inner_ref[:, hidden_size:], up_ref[piece, :], 1, 1
        )
        spread = pick_rows(slots, rows, capacity, part)
        total += dot(spread, input_grad.astype(BF16), 0, 0)
        if part == 0:
            back[:, half:] = dot(spread, score_ref[...], 0, 0).astype(BF16)
    back[:, :half] = total.astype(BF16)
    writes.append(pltpu.make_async_copy(back, back_hbm, out_sems.at[len(blocks)]))
    writes[-1].start()
    for write in writes:
        write.wait()


def expert_late(place, ring, gate, up, inner, score, inputs, scaled, hidden, capacity):
    slots, features = inputs.shape
    hidden_size = gate.shape[1]
    block = (features // (2 * ring), 3 * hidden_size)
    count = len(late_blocks(ring))
    back = (2 * slots, features // 2 + LANES)
    return pl.pallas_call(
        functools.partial(late_kernel, capacity, ring),
        in_specs=[pl.BlockSpec(memory_space=pltpu.SMEM)] + [ON_CHIP] * 7,
        out_specs=[ANYWHERE] * (1 + count),
        out_shape=[pltpu.HBM(back, BF16)] + [pltpu.HBM(block, BF16)] * count,
        scratch_shapes=[
            pltpu.VMEM((count, *block), BF16),
            pltpu.VMEM(back, BF16),
            pltpu.SemaphoreType.DMA((count + 1,)),
        ],
        compiler_params=pltpu.CompilerParams(vmem_limit_bytes=24 * 2**20),
        cost_estimate=pl.CostEstimate(
            flops=2 * slots * features * 6 * hidden_size, bytes_accessed=2**23, transcendentals=0
        ),
        name="expert_late",
    )(place, *on_chip(gate, up, inner, score, inputs, scaled, hidden))


def combine_kernel(capacity, ids_ref, slot_ref, score_ref, rows_ref, token_ref, grad_ref):
    rows = rows_ref.shape[0]
    count = token_ref.shape[0]
    half = token_ref.shape[1] // 2
    position = ids_ref[...] * (2 * capacity) + slot_ref[...]
    row = lax.broadcasted_iota(jnp.int32, (rows, count), 0)
    for part in range(2):
        pick = jnp.where(row == position + part * capacity, F32(1), F32(0)).astype(BF16)
        token_ref[:, part * half : (part + 1) * half] = dot(
            pick, rows_ref[:, :half], 0, 0
        ).astype(BF16)
        if part == 0:
            score = dot(rows_ref[:, half:], pick, 0, 0)
            grad_ref[...] = (score[0:1, :] / score_ref[...].astype(F32)).astype(BF16)


def combine(expert_ids, slot_index, gate_scores, rows, features, capacity):
    count = expert_ids.shape[0]
    return pl.pallas_call(
        functools.partial(combine_kernel, capacity),
        out_shape=[
            jax.ShapeDtypeStruct((count, features), BF16),
            jax.ShapeDtypeStruct((1, count), BF16),
        ],
        compiler_params=pltpu.CompilerParams(vmem_limit_bytes=24 * 2**20),
        name="combine",
    )(
        *in_hbm(
            expert_ids.reshape(1, count),
            slot_index.reshape(1, count),
            gate_scores.reshape(1, count),
        ),
        *on_chip(rows),
    )


def add_kernel(*refs):
    total = refs[0][...].astype(F32)
    for ref in refs[1:-1]:
        total += ref[...].astype(F32)
    refs[-1][...] = total.astype(BF16)


def add(*arrays):
    return pl.pallas_call(
        add_kernel,
        in_specs=[ON_CHIP] * len(arrays),
        out_specs=ON_CHIP,
        out_shape=pltpu.VMEM(arrays[0].shape, BF16),
        compiler_params=pltpu.CompilerParams(vmem_limit_bytes=6 * 2**20),
        name="add",
    )(*on_chip(*arrays))


def split_kernel(own_ref, up_way_ref, down_way_ref, other_ref, gate_ref, up_ref, down_ref):
    hidden_size = gate_ref.shape[1]
    total = own_ref[...].astype(F32) + up_way_ref[...].astype(F32)
    total += down_way_ref[...].astype(F32) + other_ref[...].astype(F32)
    gate_ref[...] = total[:, :hidden_size].astype(BF16)
    up_ref[...] = total[:, hidden_size : 2 * hidden_size].astype(BF16)
    down_ref[...] = total[:, 2 * hidden_size :].T.astype(BF16)


def split_grads(*parts):
    block, width = parts[0].shape
    hidden_size = width // 3
    return pl.pallas_call(
        split_kernel,
        in_specs=[ON_CHIP] * 4,
        out_shape=[
            jax.ShapeDtypeStruct((block, hidden_size), BF16),
            jax.ShapeDtypeStruct((block, hidden_size), BF16),
            jax.ShapeDtypeStruct((hidden_size, block), BF16),
        ],
        name="split_grads",
    )(*on_chip(*parts))


def ring_sums(grads, ring, back):
    far = ring // 2
    moves = {
        way: [(s * ring + i, s * ring + (i + way) % ring) for s in range(2) for i in range(ring)]
        for way in (1, -1)
    }
    block = lambda ahead, piece: grads[ahead % ring, piece]
    carried = {}
    for hop in range(far, 0, -1):
        for piece in range(2):
            for way in (1, -1):
                if hop == far and piece != (0 if way == 1 else 1):
                    continue
                own = block(way * hop, piece)
                if (way, piece) in carried:
                    own = add(own, carried[way, piece])
                carried[way, piece] = lax.ppermute(own, "dp", moves[way])
        if hop == far:
            back, *_ = lax.optimization_barrier((back, *carried.values()))
    other = lax.ppermute(
        add(block(0, 0), carried[1, 0], carried[-1, 0]),
        "dp", [(i, (i + ring) % (2 * ring)) for i in range(2 * ring)],
    )
    return back, block(0, 1), carried[1, 1], carried[-1, 1], other


def on_device(
    tokens, cotangent, gate_scores, expert_ids, slot_index, gate_weight, up_weight, down_weight
):
    experts = lax.axis_size("expert")
    count, features = tokens.shape
    capacity = 2 * count // experts
    gate, up, down = gate_weight[0], up_weight[0], down_weight[0]
    send = dispatch(expert_ids, slot_index, gate_scores, tokens, cotangent, experts, capacity)
    received = lax.all_to_all(
        send.reshape(experts, 2 * capacity, features),
        "expert", split_axis=0, concat_axis=0, tiled=True,
    ).reshape(send.shape)
    ring = lax.axis_size("dp") // 2
    index = lax.axis_index("dp")
    side = (index >= ring).astype(jnp.int32)
    place = jnp.stack([side, index - side * ring])
    held = expert_first(place, ring, received, gate, up, down, capacity)
    held, early = held[:7], held[7:]
    back, *late = expert_late(place, ring, *held, capacity)
    grads = dict(zip(early_blocks(ring) + late_blocks(ring), [*early, *late]))
    back, *parts, other = ring_sums(grads, ring, back)
    returned = lax.all_to_all(
        back.reshape(experts, 2 * capacity, back.shape[1]),
        "expert", split_axis=0, concat_axis=0, tiled=True,
    ).reshape(back.shape)
    token_grad, score_grad = combine(
        expert_ids, slot_index, gate_scores, returned, features, capacity
    )
    other, score_grad = lax.optimization_barrier((other, score_grad))
    grad_gate, grad_up, grad_down = split_grads(*parts, other)
    return token_grad, score_grad.reshape(count), grad_gate[None], grad_up[None], grad_down[None]


def solution(mesh):
    both = ("expert", "dp")
    return jax.shard_map(
        on_device,
        mesh=mesh,
        in_specs=(
            P(both, None),
            P(both, None),
            P(both),
            P(both),
            P(both),
            P("expert", None, None),
            P("expert", None, None),
            P("expert", None, None),
        ),
        out_specs=(
            P(both, None),
            P(both),
            P("expert", "dp", None),
            P("expert", "dp", None),
            P("expert", None, "dp"),
        ),
        check_vma=False,
    )
```

```python
import functools

import jax
import jax.numpy as jnp
from jax import lax
from jax.experimental import pallas as pl
from jax.experimental.pallas import tpu as pltpu
from jax.sharding import PartitionSpec as P

F32 = jnp.float32
BF16 = jnp.bfloat16
LANES = 128


def dot(left, right, left_dim, right_dim):
    return lax.dot_general(
        left, right, (((left_dim,), (right_dim,)), ((), ())), preferred_element_type=F32
    )


def in_hbm(*arrays):
    return [pltpu.with_memory_space_constraint(array, pltpu.HBM) for array in arrays]


def on_chip(*arrays):
    return [pltpu.with_memory_space_constraint(array, pltpu.VMEM) for array in arrays]


ANYWHERE = pl.BlockSpec(memory_space=pltpu.HBM)
ON_CHIP = pl.BlockSpec(memory_space=pltpu.VMEM)
CHUNKS = 4


def dispatch_kernel(
    capacity, ids_hbm, slot_hbm, score_hbm, tokens_hbm, cotan_hbm, out_hbm,
    ids_ref, slot_ref, score_ref, rows_ref, out_ref, sems, out_sems,
):
    rows, (count, features) = out_ref.shape[0], tokens_hbm.shape
    chunk = features // CHUNKS
    columns = [slice(i * chunk, (i + 1) * chunk) for i in range(CHUNKS)]
    copies = [
        pltpu.make_async_copy(ids_hbm, ids_ref, sems.at[0]),
        pltpu.make_async_copy(slot_hbm, slot_ref, sems.at[1]),
        pltpu.make_async_copy(score_hbm, score_ref, sems.at[2]),
    ]
    for i, c in enumerate(columns):
        copies += [
            pltpu.make_async_copy(tokens_hbm.at[:, c], rows_ref.at[:count, c], sems.at[3 + 2 * i]),
            pltpu.make_async_copy(cotan_hbm.at[:, c], rows_ref.at[count:, c], sems.at[4 + 2 * i]),
        ]
    for copy in copies:
        copy.start()
    for copy in copies[:3]:
        copy.wait()
    position = ids_ref[...] * (2 * capacity) + slot_ref[...]
    row = lax.broadcasted_iota(jnp.int32, (rows, count), 0)
    pick_token = jnp.where(row == position, F32(1), F32(0))
    pick_cotan = jnp.where(row == position + capacity, score_ref[...].astype(F32), F32(0))
    pick = jnp.concatenate([pick_token, pick_cotan], axis=1).astype(BF16)
    writes = []
    for i, c in enumerate(columns):
        copies[3 + 2 * i].wait()
        copies[4 + 2 * i].wait()
        out_ref[:, c] = dot(pick, rows_ref[:, c], 1, 0).astype(BF16)
        writes.append(pltpu.make_async_copy(out_ref.at[:, c], out_hbm.at[:, c], out_sems.at[i]))
        writes[-1].start()
    for write in writes:
        write.wait()


def dispatch(expert_ids, slot_index, gate_scores, tokens, cotangent, experts, capacity):
    count, features = tokens.shape
    rows = experts * 2 * capacity
    return pl.pallas_call(
        functools.partial(dispatch_kernel, capacity),
        in_specs=[ANYWHERE] * 5,
        out_specs=ANYWHERE,
        out_shape=pltpu.HBM((rows, features), BF16),
        scratch_shapes=[
            pltpu.VMEM((1, count), jnp.int32),
            pltpu.VMEM((1, count), jnp.int32),
            pltpu.VMEM((1, count), BF16),
            pltpu.VMEM((2 * count, features), BF16),
            pltpu.VMEM((rows, features), BF16),
            pltpu.SemaphoreType.DMA((3 + 2 * CHUNKS,)),
            pltpu.SemaphoreType.DMA((CHUNKS,)),
        ],
        compiler_params=pltpu.CompilerParams(vmem_limit_bytes=24 * 2**20),
        name="dispatch",
    )(
        *in_hbm(
            expert_ids.reshape(1, count),
            slot_index.reshape(1, count),
            gate_scores.reshape(1, count),
            tokens,
            cotangent,
        )
    )


def pick_rows(slots, rows, capacity, half):
    slot = lax.broadcasted_iota(jnp.int32, (slots, rows), 0)
    row = lax.broadcasted_iota(jnp.int32, (slots, rows), 1)
    wanted = (slot // capacity) * (2 * capacity) + slot % capacity + half * capacity
    return jnp.where(row == wanted, F32(1), F32(0)).astype(BF16)


def early_blocks(ring):
    far = ring // 2
    return [(far, 0), (far, 1), (far - 1, 1), (far + 1, 0)]


def late_blocks(ring):
    far = sorted(range(ring), key=lambda k: -min(k, ring - k))
    return [(k, p) for k in far for p in range(2) if (k, p) not in early_blocks(ring)]


def write_blocks(blocks, ring, place_ref, inputs, scaled, inner, hidden, stage, outs, sems):
    side, spot = place_ref[0], place_ref[1]
    block = inputs.shape[1] // (2 * ring)
    hidden_size = hidden.shape[1]
    writes = []
    for i, (ahead, piece) in enumerate(blocks):
        owner = side if piece else 1 - side
        column = owner * ring + lax.rem(spot + ahead, ring)
        columns = pl.ds(pl.multiple_of(column * block, block), block)
        stage[i, :, : 2 * hidden_size] = dot(inputs[:, columns], inner[...], 0, 0).astype(BF16)
        stage[i, :, 2 * hidden_size :] = dot(scaled[:, columns], hidden[...], 0, 0).astype(BF16)
        writes.append(pltpu.make_async_copy(stage.at[i], outs[i], sems.at[i]))
        writes[-1].start()
    return writes


def expert_kernel(
    capacity, ring, place_ref, recv_ref, gate_hbm, up_hbm, down_hbm,
    gate_ref, up_ref, inner_ref, score_ref, inputs, scaled, hidden_ref, *rest,
):
    blocks = early_blocks(ring)
    grads, (down_ref, stage, sems, out_sems) = rest[: len(blocks)], rest[len(blocks) :]
    rows, features = recv_ref.shape
    slots = rows // 2
    hidden_size = gate_ref.shape[1]
    copies = [
        pltpu.make_async_copy(source, target, sems.at[i])
        for i, (source, target) in enumerate(
            ((gate_hbm, gate_ref), (up_hbm, up_ref), (down_hbm, down_ref))
        )
    ]
    for copy in copies:
        copy.start()
    received = recv_ref[...]
    inputs[...] = dot(pick_rows(slots, rows, capacity, 0), received, 1, 0).astype(BF16)
    scaled[...] = dot(pick_rows(slots, rows, capacity, 1), received, 1, 0).astype(BF16)
    copies[0].wait()
    pre_gate = dot(inputs[...], gate_ref[...], 1, 0)
    copies[1].wait()
    pre_up = dot(inputs[...], up_ref[...], 1, 0)
    copies[2].wait()
    hidden_grad = dot(scaled[...], down_ref[...], 1, 1)
    sigmoid = jax.nn.sigmoid(pre_gate)
    activated = pre_gate * sigmoid
    hidden = (activated * pre_up).astype(BF16)
    hidden_ref[...] = hidden
    inner_ref[:, :hidden_size] = (
        hidden_grad * pre_up * sigmoid * (1.0 + pre_gate * (1.0 - sigmoid))
    ).astype(BF16)
    inner_ref[:, hidden_size:] = (hidden_grad * activated).astype(BF16)
    score = jnp.sum(hidden.astype(F32) * hidden_grad, axis=1, keepdims=True)
    score_ref[...] = jnp.broadcast_to(score, score_ref.shape).astype(BF16)
    for write in write_blocks(
        blocks, ring, place_ref, inputs, scaled, inner_ref, hidden_ref, stage, grads, out_sems
    ):
        write.wait()


def expert_first(place, ring, received, gate, up, down, capacity):
    rows, features = received.shape
    hidden_size = gate.shape[1]
    slots = rows // 2
    block = (features // (2 * ring), 3 * hidden_size)
    count = len(early_blocks(ring))
    return pl.pallas_call(
        functools.partial(expert_kernel, capacity, ring),
        in_specs=[pl.BlockSpec(memory_space=pltpu.SMEM), ON_CHIP, ANYWHERE, ANYWHERE, ANYWHERE],
        out_specs=[ON_CHIP] * 7 + [ANYWHERE] * count,
        out_shape=[
            pltpu.VMEM(gate.shape, BF16),
            pltpu.VMEM(up.shape, BF16),
            pltpu.VMEM((slots, 2 * hidden_size), BF16),
            pltpu.VMEM((slots, LANES), BF16),
            pltpu.VMEM((slots, features), BF16),
            pltpu.VMEM((slots, features), BF16),
            pltpu.VMEM((slots, hidden_size), BF16),
        ]
        + [pltpu.HBM(block, BF16)] * count,
        scratch_shapes=[
            pltpu.VMEM(down.shape, BF16),
            pltpu.VMEM((count, *block), BF16),
            pltpu.SemaphoreType.DMA((3,)),
            pltpu.SemaphoreType.DMA((count,)),
        ],
        compiler_params=pltpu.CompilerParams(vmem_limit_bytes=24 * 2**20),
        name="expert_first",
    )(place, *on_chip(received), *in_hbm(gate, up, down))


def late_kernel(
    capacity, ring, place_ref, gate_ref, up_ref, inner_ref, score_ref, inputs, scaled, hidden_ref,
    back_hbm, *rest,
):
    blocks = late_blocks(ring)
    grads, (stage, back, out_sems) = rest[: len(blocks)], rest[len(blocks) :]
    slots = inner_ref.shape[0]
    rows = back.shape[0]
    hidden_size = gate_ref.shape[1]
    half = gate_ref.shape[0] // 2
    writes = write_blocks(
        blocks, ring, place_ref, inputs, scaled, inner_ref, hidden_ref, stage, grads, out_sems
    )
    total = jnp.zeros((rows, half), F32)
    for part in range(2):
        piece = pl.ds(part * half, half)
        input_grad = dot(inner_ref[:, :hidden_size], gate_ref[piece, :], 1, 1) + dot(
            inner_ref[:, hidden_size:], up_ref[piece, :], 1, 1
        )
        spread = pick_rows(slots, rows, capacity, part)
        total += dot(spread, input_grad.astype(BF16), 0, 0)
        if part == 0:
            back[:, half:] = dot(spread, score_ref[...], 0, 0).astype(BF16)
    back[:, :half] = total.astype(BF16)
    writes.append(pltpu.make_async_copy(back, back_hbm, out_sems.at[len(blocks)]))
    writes[-1].start()
    for write in writes:
        write.wait()


def expert_late(place, ring, gate, up, inner, score, inputs, scaled, hidden, capacity):
    slots, features = inputs.shape
    hidden_size = gate.shape[1]
    block = (features // (2 * ring), 3 * hidden_size)
    count = len(late_blocks(ring))
    back = (2 * slots, features // 2 + LANES)
    return pl.pallas_call(
        functools.partial(late_kernel, capacity, ring),
        in_specs=[pl.BlockSpec(memory_space=pltpu.SMEM)] + [ON_CHIP] * 7,
        out_specs=[ANYWHERE] * (1 + count),
        out_shape=[pltpu.HBM(back, BF16)] + [pltpu.HBM(block, BF16)] * count,
        scratch_shapes=[
            pltpu.VMEM((count, *block), BF16),
            pltpu.VMEM(back, BF16),
            pltpu.SemaphoreType.DMA((count + 1,)),
        ],
        compiler_params=pltpu.CompilerParams(vmem_limit_bytes=24 * 2**20),
        cost_estimate=pl.CostEstimate(
            flops=2 * slots * features * 6 * hidden_size, bytes_accessed=2**23, transcendentals=0
        ),
        name="expert_late",
    )(place, *on_chip(gate, up, inner, score, inputs, scaled, hidden))


def combine_kernel(capacity, ids_ref, slot_ref, score_ref, rows_ref, token_ref, grad_ref):
    rows = rows_ref.shape[0]
    count = token_ref.shape[0]
    half = token_ref.shape[1] // 2
    position = ids_ref[...] * (2 * capacity) + slot_ref[...]
    row = lax.broadcasted_iota(jnp.int32, (rows, count), 0)
    for part in range(2):
        pick = jnp.where(row == position + part * capacity, F32(1), F32(0)).astype(BF16)
        token_ref[:, part * half : (part + 1) * half] = dot(
            pick, rows_ref[:, :half], 0, 0
        ).astype(BF16)
        if part == 0:
            score = dot(rows_ref[:, half:], pick, 0, 0)
            grad_ref[...] = (score[0:1, :] / score_ref[...].astype(F32)).astype(BF16)


def combine(expert_ids, slot_index, gate_scores, rows, features, capacity):
    count = expert_ids.shape[0]
    return pl.pallas_call(
        functools.partial(combine_kernel, capacity),
        out_shape=[
            jax.ShapeDtypeStruct((count, features), BF16),
            jax.ShapeDtypeStruct((1, count), BF16),
        ],
        compiler_params=pltpu.CompilerParams(vmem_limit_bytes=24 * 2**20),
        name="combine",
    )(
        *in_hbm(
            expert_ids.reshape(1, count),
            slot_index.reshape(1, count),
            gate_scores.reshape(1, count),
        ),
        *on_chip(rows),
    )


def add_kernel(*refs):
    total = refs[0][...].astype(F32)
    for ref in refs[1:-1]:
        total += ref[...].astype(F32)
    refs[-1][...] = total.astype(BF16)


def add(*arrays):
    return pl.pallas_call(
        add_kernel,
        in_specs=[ON_CHIP] * len(arrays),
        out_specs=ON_CHIP,
        out_shape=pltpu.VMEM(arrays[0].shape, BF16),
        compiler_params=pltpu.CompilerParams(vmem_limit_bytes=6 * 2**20),
        name="add",
    )(*on_chip(*arrays))


def split_kernel(own_ref, up_way_ref, down_way_ref, other_ref, gate_ref, up_ref, down_ref):
    hidden_size = gate_ref.shape[1]
    total = own_ref[...].astype(F32) + up_way_ref[...].astype(F32)
    total += down_way_ref[...].astype(F32) + other_ref[...].astype(F32)
    gate_ref[...] = total[:, :hidden_size].astype(BF16)
    up_ref[...] = total[:, hidden_size : 2 * hidden_size].astype(BF16)
    down_ref[...] = total[:, 2 * hidden_size :].T.astype(BF16)


def split_grads(*parts):
    block, width = parts[0].shape
    hidden_size = width // 3
    return pl.pallas_call(
        split_kernel,
        in_specs=[ON_CHIP] * 4,
        out_shape=[
            jax.ShapeDtypeStruct((block, hidden_size), BF16),
            jax.ShapeDtypeStruct((block, hidden_size), BF16),
            jax.ShapeDtypeStruct((hidden_size, block), BF16),
        ],
        name="split_grads",
    )(*on_chip(*parts))


def ring_sums(grads, ring, back):
    far = ring // 2
    moves = {
        way: [(s * ring + i, s * ring + (i + way) % ring) for s in range(2) for i in range(ring)]
        for way in (1, -1)
    }
    block = lambda ahead, piece: grads[ahead % ring, piece]
    carried, first = {}, []
    for hop in range(far, 0, -1):
        for piece in range(2):
            for way in (1, -1):
                if hop == far and piece != (0 if way == 1 else 1):
                    continue
                own = block(way * hop, piece)
                fresh = (way, piece) not in carried
                if not fresh:
                    own = add(own, carried[way, piece])
                carried[way, piece] = lax.ppermute(own, "dp", moves[way])
                if fresh:
                    first.append(carried[way, piece])
        if hop == far - 1:
            back, *_ = lax.optimization_barrier((back, *first))
    other = lax.ppermute(
        add(block(0, 0), carried[1, 0], carried[-1, 0]),
        "dp", [(i, (i + ring) % (2 * ring)) for i in range(2 * ring)],
    )
    return back, block(0, 1), carried[1, 1], carried[-1, 1], other


def on_device(
    tokens, cotangent, gate_scores, expert_ids, slot_index, gate_weight, up_weight, down_weight
):
    experts = lax.axis_size("expert")
    count, features = tokens.shape
    capacity = 2 * count // experts
    gate, up, down = gate_weight[0], up_weight[0], down_weight[0]
    send = dispatch(expert_ids, slot_index, gate_scores, tokens, cotangent, experts, capacity)
    received = lax.all_to_all(
        send.reshape(experts, 2 * capacity, features),
        "expert", split_axis=0, concat_axis=0, tiled=True,
    ).reshape(send.shape)
    ring = lax.axis_size("dp") // 2
    index = lax.axis_index("dp")
    side = (index >= ring).astype(jnp.int32)
    place = jnp.stack([side, index - side * ring])
    held = expert_first(place, ring, received, gate, up, down, capacity)
    held, early = held[:7], held[7:]
    back, *late = expert_late(place, ring, *held, capacity)
    grads = dict(zip(early_blocks(ring) + late_blocks(ring), [*early, *late]))
    back, *parts, other = ring_sums(grads, ring, back)
    returned = lax.all_to_all(
        back.reshape(experts, 2 * capacity, back.shape[1]),
        "expert", split_axis=0, concat_axis=0, tiled=True,
    ).reshape(back.shape)
    token_grad, score_grad = combine(
        expert_ids, slot_index, gate_scores, returned, features, capacity
    )
    other, score_grad = lax.optimization_barrier((other, score_grad))
    grad_gate, grad_up, grad_down = split_grads(*parts, other)
    return token_grad, score_grad.reshape(count), grad_gate[None], grad_up[None], grad_down[None]


def solution(mesh):
    both = ("expert", "dp")
    return jax.shard_map(
        on_device,
        mesh=mesh,
        in_specs=(
            P(both, None),
            P(both, None),
            P(both),
            P(both),
            P(both),
            P("expert", None, None),
            P("expert", None, None),
            P("expert", None, None),
        ),
        out_specs=(
            P(both, None),
            P(both),
            P("expert", "dp", None),
            P("expert", "dp", None),
            P("expert", None, "dp"),
        ),
        check_vma=False,
    )
```

```python
import functools

import jax
import jax.numpy as jnp
from jax import lax
from jax.experimental import pallas as pl
from jax.experimental.pallas import tpu as pltpu
from jax.sharding import PartitionSpec as P

F32 = jnp.float32
BF16 = jnp.bfloat16
LANES = 128


def dot(left, right, left_dim, right_dim):
    return lax.dot_general(
        left, right, (((left_dim,), (right_dim,)), ((), ())), preferred_element_type=F32
    )


def in_hbm(*arrays):
    return [pltpu.with_memory_space_constraint(array, pltpu.HBM) for array in arrays]


def on_chip(*arrays):
    return [pltpu.with_memory_space_constraint(array, pltpu.VMEM) for array in arrays]


ANYWHERE = pl.BlockSpec(memory_space=pltpu.HBM)
ON_CHIP = pl.BlockSpec(memory_space=pltpu.VMEM)
CHUNKS = 4


def dispatch_kernel(
    capacity, ids_hbm, slot_hbm, score_hbm, tokens_hbm, cotan_hbm, out_hbm,
    ids_ref, slot_ref, score_ref, rows_ref, out_ref, sems, out_sems,
):
    rows, (count, features) = out_ref.shape[0], tokens_hbm.shape
    chunk = features // CHUNKS
    columns = [slice(i * chunk, (i + 1) * chunk) for i in range(CHUNKS)]
    copies = [
        pltpu.make_async_copy(ids_hbm, ids_ref, sems.at[0]),
        pltpu.make_async_copy(slot_hbm, slot_ref, sems.at[1]),
        pltpu.make_async_copy(score_hbm, score_ref, sems.at[2]),
    ]
    for i, c in enumerate(columns):
        copies += [
            pltpu.make_async_copy(tokens_hbm.at[:, c], rows_ref.at[:count, c], sems.at[3 + 2 * i]),
            pltpu.make_async_copy(cotan_hbm.at[:, c], rows_ref.at[count:, c], sems.at[4 + 2 * i]),
        ]
    for copy in copies:
        copy.start()
    for copy in copies[:3]:
        copy.wait()
    position = ids_ref[...] * (2 * capacity) + slot_ref[...]
    row = lax.broadcasted_iota(jnp.int32, (rows, count), 0)
    pick_token = jnp.where(row == position, F32(1), F32(0))
    pick_cotan = jnp.where(row == position + capacity, score_ref[...].astype(F32), F32(0))
    pick = jnp.concatenate([pick_token, pick_cotan], axis=1).astype(BF16)
    writes = []
    for i, c in enumerate(columns):
        copies[3 + 2 * i].wait()
        copies[4 + 2 * i].wait()
        out_ref[:, c] = dot(pick, rows_ref[:, c], 1, 0).astype(BF16)
        writes.append(pltpu.make_async_copy(out_ref.at[:, c], out_hbm.at[:, c], out_sems.at[i]))
        writes[-1].start()
    for write in writes:
        write.wait()


def dispatch(expert_ids, slot_index, gate_scores, tokens, cotangent, experts, capacity):
    count, features = tokens.shape
    rows = experts * 2 * capacity
    return pl.pallas_call(
        functools.partial(dispatch_kernel, capacity),
        in_specs=[ANYWHERE] * 5,
        out_specs=ANYWHERE,
        out_shape=pltpu.HBM((rows, features), BF16),
        scratch_shapes=[
            pltpu.VMEM((1, count), jnp.int32),
            pltpu.VMEM((1, count), jnp.int32),
            pltpu.VMEM((1, count), BF16),
            pltpu.VMEM((2 * count, features), BF16),
            pltpu.VMEM((rows, features), BF16),
            pltpu.SemaphoreType.DMA((3 + 2 * CHUNKS,)),
            pltpu.SemaphoreType.DMA((CHUNKS,)),
        ],
        compiler_params=pltpu.CompilerParams(vmem_limit_bytes=24 * 2**20),
        name="dispatch",
    )(
        *in_hbm(
            expert_ids.reshape(1, count),
            slot_index.reshape(1, count),
            gate_scores.reshape(1, count),
            tokens,
            cotangent,
        )
    )


def pick_rows(slots, rows, capacity, half):
    slot = lax.broadcasted_iota(jnp.int32, (slots, rows), 0)
    row = lax.broadcasted_iota(jnp.int32, (slots, rows), 1)
    wanted = (slot // capacity) * (2 * capacity) + slot % capacity + half * capacity
    return jnp.where(row == wanted, F32(1), F32(0)).astype(BF16)


def early_blocks(ring):
    far = ring // 2
    return [(far, 0), (far, 1), (far - 1, 1), (far + 1, 0)]


def late_blocks(ring):
    far = sorted(range(ring), key=lambda k: -min(k, ring - k))
    return [(k, p) for k in far for p in range(2) if (k, p) not in early_blocks(ring)]


def write_blocks(blocks, ring, place_ref, inputs, scaled, inner, hidden, stage, outs, sems):
    side, spot = place_ref[0], place_ref[1]
    block = inputs.shape[1] // (2 * ring)
    hidden_size = hidden.shape[1]
    writes = []
    for i, (ahead, piece) in enumerate(blocks):
        owner = side if piece else 1 - side
        column = owner * ring + lax.rem(spot + ahead, ring)
        columns = pl.ds(pl.multiple_of(column * block, block), block)
        stage[i, :, : 2 * hidden_size] = dot(inputs[:, columns], inner[...], 0, 0).astype(BF16)
        stage[i, :, 2 * hidden_size :] = dot(scaled[:, columns], hidden[...], 0, 0).astype(BF16)
        writes.append(pltpu.make_async_copy(stage.at[i], outs[i], sems.at[i]))
        writes[-1].start()
    return writes


def expert_kernel(
    capacity, ring, place_ref, recv_ref, gate_hbm, up_hbm, down_hbm,
    inner_ref, inputs, scaled, hidden_ref, back_hbm, *rest,
):
    blocks = early_blocks(ring)
    grads, scratch = rest[: len(blocks)], rest[len(blocks) :]
    gate_ref, up_ref, down_ref, stage, back, sems, out_sems = scratch
    rows, features = recv_ref.shape
    slots = rows // 2
    hidden_size = gate_ref.shape[1]
    copies = [
        pltpu.make_async_copy(source, target, sems.at[i])
        for i, (source, target) in enumerate(
            ((gate_hbm, gate_ref), (up_hbm, up_ref), (down_hbm, down_ref))
        )
    ]
    for copy in copies:
        copy.start()
    received = recv_ref[...]
    inputs[...] = dot(pick_rows(slots, rows, capacity, 0), received, 1, 0).astype(BF16)
    scaled[...] = dot(pick_rows(slots, rows, capacity, 1), received, 1, 0).astype(BF16)
    copies[0].wait()
    pre_gate = dot(inputs[...], gate_ref[...], 1, 0)
    copies[1].wait()
    pre_up = dot(inputs[...], up_ref[...], 1, 0)
    copies[2].wait()
    hidden_grad = dot(scaled[...], down_ref[...], 1, 1)
    sigmoid = jax.nn.sigmoid(pre_gate)
    activated = pre_gate * sigmoid
    hidden = (activated * pre_up).astype(BF16)
    hidden_ref[...] = hidden
    inner_ref[:, :hidden_size] = (
        hidden_grad * pre_up * sigmoid * (1.0 + pre_gate * (1.0 - sigmoid))
    ).astype(BF16)
    inner_ref[:, hidden_size:] = (hidden_grad * activated).astype(BF16)
    score = jnp.sum(hidden.astype(F32) * hidden_grad, axis=1, keepdims=True)
    score = jnp.broadcast_to(score, (slots, LANES)).astype(BF16)
    writes = write_blocks(
        blocks, ring, place_ref, inputs, scaled, inner_ref, hidden_ref, stage, grads, out_sems
    )
    half = features // 2
    total = jnp.zeros((rows, half), F32)
    for part in range(2):
        piece = pl.ds(part * half, half)
        input_grad = dot(inner_ref[:, :hidden_size], gate_ref[piece, :], 1, 1) + dot(
            inner_ref[:, hidden_size:], up_ref[piece, :], 1, 1
        )
        spread = pick_rows(slots, rows, capacity, part)
        total += dot(spread, input_grad.astype(BF16), 0, 0)
        if part == 0:
            back[:, half:] = dot(spread, score, 0, 0).astype(BF16)
    back[:, :half] = total.astype(BF16)
    writes.append(pltpu.make_async_copy(back, back_hbm, out_sems.at[len(blocks)]))
    writes[-1].start()
    for write in writes:
        write.wait()


def expert_first(place, ring, received, gate, up, down, capacity):
    rows, features = received.shape
    hidden_size = gate.shape[1]
    slots = rows // 2
    block = (features // (2 * ring), 3 * hidden_size)
    count = len(early_blocks(ring))
    back = (rows, features // 2 + LANES)
    return pl.pallas_call(
        functools.partial(expert_kernel, capacity, ring),
        in_specs=[pl.BlockSpec(memory_space=pltpu.SMEM), ON_CHIP, ANYWHERE, ANYWHERE, ANYWHERE],
        out_specs=[ON_CHIP] * 4 + [ANYWHERE] * (1 + count),
        out_shape=[
            pltpu.VMEM((slots, 2 * hidden_size), BF16),
            pltpu.VMEM((slots, features), BF16),
            pltpu.VMEM((slots, features), BF16),
            pltpu.VMEM((slots, hidden_size), BF16),
            pltpu.HBM(back, BF16),
        ]
        + [pltpu.HBM(block, BF16)] * count,
        scratch_shapes=[
            pltpu.VMEM(gate.shape, BF16),
            pltpu.VMEM(up.shape, BF16),
            pltpu.VMEM(down.shape, BF16),
            pltpu.VMEM((count, *block), BF16),
            pltpu.VMEM(back, BF16),
            pltpu.SemaphoreType.DMA((3,)),
            pltpu.SemaphoreType.DMA((count + 1,)),
        ],
        compiler_params=pltpu.CompilerParams(vmem_limit_bytes=24 * 2**20),
        name="expert_first",
    )(place, *on_chip(received), *in_hbm(gate, up, down))


def late_kernel(
    ring, place_ref, inner_ref, inputs, scaled, hidden_ref, *rest
):
    blocks = late_blocks(ring)
    grads, (stage, out_sems) = rest[: len(blocks)], rest[len(blocks) :]
    writes = write_blocks(
        blocks, ring, place_ref, inputs, scaled, inner_ref, hidden_ref, stage, grads, out_sems
    )
    for write in writes:
        write.wait()


def expert_late(place, ring, inner, inputs, scaled, hidden):
    slots, features = inputs.shape
    hidden_size = hidden.shape[1]
    block = (features // (2 * ring), 3 * hidden_size)
    count = len(late_blocks(ring))
    return pl.pallas_call(
        functools.partial(late_kernel, ring),
        in_specs=[pl.BlockSpec(memory_space=pltpu.SMEM)] + [ON_CHIP] * 4,
        out_specs=[ANYWHERE] * count,
        out_shape=[pltpu.HBM(block, BF16)] * count,
        scratch_shapes=[
            pltpu.VMEM((count, *block), BF16),
            pltpu.SemaphoreType.DMA((count,)),
        ],
        compiler_params=pltpu.CompilerParams(vmem_limit_bytes=16 * 2**20),
        name="expert_late",
    )(place, *on_chip(inner, inputs, scaled, hidden))


def combine_kernel(capacity, ids_ref, slot_ref, score_ref, rows_ref, token_ref, grad_ref):
    rows = rows_ref.shape[0]
    count = token_ref.shape[0]
    half = token_ref.shape[1] // 2
    position = ids_ref[...] * (2 * capacity) + slot_ref[...]
    row = lax.broadcasted_iota(jnp.int32, (rows, count), 0)
    for part in range(2):
        pick = jnp.where(row == position + part * capacity, F32(1), F32(0)).astype(BF16)
        token_ref[:, part * half : (part + 1) * half] = dot(
            pick, rows_ref[:, :half], 0, 0
        ).astype(BF16)
        if part == 0:
            score = dot(rows_ref[:, half:], pick, 0, 0)
            grad_ref[...] = (score[0:1, :] / score_ref[...].astype(F32)).astype(BF16)


def combine(expert_ids, slot_index, gate_scores, rows, features, capacity):
    count = expert_ids.shape[0]
    return pl.pallas_call(
        functools.partial(combine_kernel, capacity),
        out_shape=[
            jax.ShapeDtypeStruct((count, features), BF16),
            jax.ShapeDtypeStruct((1, count), BF16),
        ],
        compiler_params=pltpu.CompilerParams(vmem_limit_bytes=24 * 2**20),
        name="combine",
    )(
        *in_hbm(
            expert_ids.reshape(1, count),
            slot_index.reshape(1, count),
            gate_scores.reshape(1, count),
        ),
        *on_chip(rows),
    )


def add_kernel(*refs):
    total = refs[0][...].astype(F32)
    for ref in refs[1:-1]:
        total += ref[...].astype(F32)
    refs[-1][...] = total.astype(BF16)


def add(*arrays):
    return pl.pallas_call(
        add_kernel,
        in_specs=[ON_CHIP] * len(arrays),
        out_specs=ON_CHIP,
        out_shape=pltpu.VMEM(arrays[0].shape, BF16),
        compiler_params=pltpu.CompilerParams(vmem_limit_bytes=6 * 2**20),
        name="add",
    )(*on_chip(*arrays))


def split_kernel(own_ref, up_way_ref, down_way_ref, other_ref, gate_ref, up_ref, down_ref):
    hidden_size = gate_ref.shape[1]
    total = own_ref[...].astype(F32) + up_way_ref[...].astype(F32)
    total += down_way_ref[...].astype(F32) + other_ref[...].astype(F32)
    gate_ref[...] = total[:, :hidden_size].astype(BF16)
    up_ref[...] = total[:, hidden_size : 2 * hidden_size].astype(BF16)
    down_ref[...] = total[:, 2 * hidden_size :].T.astype(BF16)


def split_grads(*parts):
    block, width = parts[0].shape
    hidden_size = width // 3
    return pl.pallas_call(
        split_kernel,
        in_specs=[ON_CHIP] * 4,
        out_shape=[
            jax.ShapeDtypeStruct((block, hidden_size), BF16),
            jax.ShapeDtypeStruct((block, hidden_size), BF16),
            jax.ShapeDtypeStruct((hidden_size, block), BF16),
        ],
        name="split_grads",
    )(*on_chip(*parts))


def ring_sums(grads, ring):
    far = ring // 2
    moves = {
        way: [(s * ring + i, s * ring + (i + way) % ring) for s in range(2) for i in range(ring)]
        for way in (1, -1)
    }
    block = lambda ahead, piece: grads[ahead % ring, piece]
    carried = {}
    for hop in range(far, 0, -1):
        for piece in range(2):
            for way in (1, -1):
                if hop == far and piece != (0 if way == 1 else 1):
                    continue
                own = block(way * hop, piece)
                if (way, piece) in carried:
                    own = add(own, carried[way, piece])
                carried[way, piece] = lax.ppermute(own, "dp", moves[way])
    other = lax.ppermute(
        add(block(0, 0), carried[1, 0], carried[-1, 0]),
        "dp", [(i, (i + ring) % (2 * ring)) for i in range(2 * ring)],
    )
    return block(0, 1), carried[1, 1], carried[-1, 1], other


def on_device(
    tokens, cotangent, gate_scores, expert_ids, slot_index, gate_weight, up_weight, down_weight
):
    experts = lax.axis_size("expert")
    count, features = tokens.shape
    capacity = 2 * count // experts
    gate, up, down = gate_weight[0], up_weight[0], down_weight[0]
    send = dispatch(expert_ids, slot_index, gate_scores, tokens, cotangent, experts, capacity)
    received = lax.all_to_all(
        send.reshape(experts, 2 * capacity, features),
        "expert", split_axis=0, concat_axis=0, tiled=True,
    ).reshape(send.shape)
    ring = lax.axis_size("dp") // 2
    index = lax.axis_index("dp")
    side = (index >= ring).astype(jnp.int32)
    place = jnp.stack([side, index - side * ring])
    *held, back, f0, f1, f2, f3 = expert_first(place, ring, received, gate, up, down, capacity)
    late = expert_late(place, ring, *held)
    grads = dict(zip(early_blocks(ring) + late_blocks(ring), [f0, f1, f2, f3, *late]))
    *parts, other = ring_sums(grads, ring)
    returned = lax.all_to_all(
        back.reshape(experts, 2 * capacity, back.shape[1]),
        "expert", split_axis=0, concat_axis=0, tiled=True,
    ).reshape(back.shape)
    token_grad, score_grad = combine(
        expert_ids, slot_index, gate_scores, returned, features, capacity
    )
    other, score_grad = lax.optimization_barrier((other, score_grad))
    grad_gate, grad_up, grad_down = split_grads(*parts, other)
    return token_grad, score_grad.reshape(count), grad_gate[None], grad_up[None], grad_down[None]


def solution(mesh):
    both = ("expert", "dp")
    return jax.shard_map(
        on_device,
        mesh=mesh,
        in_specs=(
            P(both, None),
            P(both, None),
            P(both),
            P(both),
            P(both),
            P("expert", None, None),
            P("expert", None, None),
            P("expert", None, None),
        ),
        out_specs=(
            P(both, None),
            P(both),
            P("expert", "dp", None),
            P("expert", "dp", None),
            P("expert", None, "dp"),
        ),
        check_vma=False,
    )
```

```python
import functools

import jax
import jax.numpy as jnp
from jax import lax
from jax.experimental import pallas as pl
from jax.experimental.pallas import tpu as pltpu
from jax.sharding import PartitionSpec as P

F32 = jnp.float32
BF16 = jnp.bfloat16
LANES = 128


def dot(left, right, left_dim, right_dim):
    return lax.dot_general(
        left, right, (((left_dim,), (right_dim,)), ((), ())), preferred_element_type=F32
    )


def in_hbm(*arrays):
    return [pltpu.with_memory_space_constraint(array, pltpu.HBM) for array in arrays]


def on_chip(*arrays):
    return [pltpu.with_memory_space_constraint(array, pltpu.VMEM) for array in arrays]


ANYWHERE = pl.BlockSpec(memory_space=pltpu.HBM)
ON_CHIP = pl.BlockSpec(memory_space=pltpu.VMEM)
CHUNKS = 4


def dispatch_kernel(
    capacity, ids_hbm, slot_hbm, score_hbm, tokens_hbm, cotan_hbm, out_hbm,
    ids_ref, slot_ref, score_ref, rows_ref, out_ref, sems, out_sems,
):
    rows, (count, features) = out_ref.shape[0], tokens_hbm.shape
    chunk = features // CHUNKS
    columns = [slice(i * chunk, (i + 1) * chunk) for i in range(CHUNKS)]
    copies = [
        pltpu.make_async_copy(ids_hbm, ids_ref, sems.at[0]),
        pltpu.make_async_copy(slot_hbm, slot_ref, sems.at[1]),
        pltpu.make_async_copy(score_hbm, score_ref, sems.at[2]),
    ]
    for i, c in enumerate(columns):
        copies += [
            pltpu.make_async_copy(tokens_hbm.at[:, c], rows_ref.at[:count, c], sems.at[3 + 2 * i]),
            pltpu.make_async_copy(cotan_hbm.at[:, c], rows_ref.at[count:, c], sems.at[4 + 2 * i]),
        ]
    for copy in copies:
        copy.start()
    for copy in copies[:3]:
        copy.wait()
    position = ids_ref[...] * (2 * capacity) + slot_ref[...]
    row = lax.broadcasted_iota(jnp.int32, (rows, count), 0)
    pick_token = jnp.where(row == position, F32(1), F32(0))
    pick_cotan = jnp.where(row == position + capacity, score_ref[...].astype(F32), F32(0))
    pick = jnp.concatenate([pick_token, pick_cotan], axis=1).astype(BF16)
    writes = []
    for i, c in enumerate(columns):
        copies[3 + 2 * i].wait()
        copies[4 + 2 * i].wait()
        out_ref[:, c] = dot(pick, rows_ref[:, c], 1, 0).astype(BF16)
        writes.append(pltpu.make_async_copy(out_ref.at[:, c], out_hbm.at[:, c], out_sems.at[i]))
        writes[-1].start()
    for write in writes:
        write.wait()


def dispatch(expert_ids, slot_index, gate_scores, tokens, cotangent, experts, capacity):
    count, features = tokens.shape
    rows = experts * 2 * capacity
    return pl.pallas_call(
        functools.partial(dispatch_kernel, capacity),
        in_specs=[ANYWHERE] * 5,
        out_specs=ANYWHERE,
        out_shape=pltpu.HBM((rows, features), BF16),
        scratch_shapes=[
            pltpu.VMEM((1, count), jnp.int32),
            pltpu.VMEM((1, count), jnp.int32),
            pltpu.VMEM((1, count), BF16),
            pltpu.VMEM((2 * count, features), BF16),
            pltpu.VMEM((rows, features), BF16),
            pltpu.SemaphoreType.DMA((3 + 2 * CHUNKS,)),
            pltpu.SemaphoreType.DMA((CHUNKS,)),
        ],
        compiler_params=pltpu.CompilerParams(vmem_limit_bytes=24 * 2**20),
        name="dispatch",
    )(
        *in_hbm(
            expert_ids.reshape(1, count),
            slot_index.reshape(1, count),
            gate_scores.reshape(1, count),
            tokens,
            cotangent,
        )
    )


def pick_rows(slots, rows, capacity, half):
    slot = lax.broadcasted_iota(jnp.int32, (slots, rows), 0)
    row = lax.broadcasted_iota(jnp.int32, (slots, rows), 1)
    wanted = (slot // capacity) * (2 * capacity) + slot % capacity + half * capacity
    return jnp.where(row == wanted, F32(1), F32(0)).astype(BF16)


def expert_kernel(
    capacity, ring, place_ref, recv_ref, gate_hbm, up_hbm, down_hbm,
    gate_ref, up_ref, inner_ref, score_ref, *rest,
):
    grads, scratch = rest[: 2 * ring], rest[2 * ring :]
    down_ref, inputs, scaled, hidden_sc, stage, sems, out_sems = scratch
    rows, features = recv_ref.shape
    slots = rows // 2
    hidden_size = gate_ref.shape[1]
    side, spot = place_ref[0], place_ref[1]
    copies = [
        pltpu.make_async_copy(source, target, sems.at[i])
        for i, (source, target) in enumerate(
            ((gate_hbm, gate_ref), (up_hbm, up_ref), (down_hbm, down_ref))
        )
    ]
    for copy in copies:
        copy.start()
    received = recv_ref[...]
    inputs[...] = dot(pick_rows(slots, rows, capacity, 0), received, 1, 0).astype(BF16)
    scaled[...] = dot(pick_rows(slots, rows, capacity, 1), received, 1, 0).astype(BF16)
    copies[0].wait()
    pre_gate = dot(inputs[...], gate_ref[...], 1, 0)
    copies[1].wait()
    pre_up = dot(inputs[...], up_ref[...], 1, 0)
    copies[2].wait()
    hidden_grad = dot(scaled[...], down_ref[...], 1, 1)
    sigmoid = jax.nn.sigmoid(pre_gate)
    activated = pre_gate * sigmoid
    hidden = (activated * pre_up).astype(BF16)
    hidden_sc[...] = hidden
    inner_ref[:, :hidden_size] = (
        hidden_grad * pre_up * sigmoid * (1.0 + pre_gate * (1.0 - sigmoid))
    ).astype(BF16)
    inner_ref[:, hidden_size:] = (hidden_grad * activated).astype(BF16)
    score = jnp.sum(hidden.astype(F32) * hidden_grad, axis=1, keepdims=True)
    score_ref[...] = jnp.broadcast_to(score, score_ref.shape).astype(BF16)

    block = features // (2 * ring)
    writes = []
    for ahead in sorted(range(ring), key=lambda k: -min(k, ring - k)):
        for piece in range(2):
            owner = side if piece else 1 - side
            column = owner * ring + lax.rem(spot + ahead, ring)
            columns = pl.ds(pl.multiple_of(column * block, block), block)
            which = 2 * ahead + piece
            stage[which, :, : 2 * hidden_size] = dot(
                inputs[:, columns], inner_ref[...], 0, 0
            ).astype(BF16)
            stage[which, :, 2 * hidden_size :] = dot(
                scaled[:, columns], hidden_sc[...], 0, 0
            ).astype(BF16)
            writes.append(pltpu.make_async_copy(stage.at[which], grads[which], out_sems.at[which]))
            writes[-1].start()
    for write in writes:
        write.wait()


def expert_grads(place, ring, received, gate, up, down, capacity):
    rows, features = received.shape
    hidden_size = gate.shape[1]
    slots = rows // 2
    block = (features // (2 * ring), 3 * hidden_size)
    return pl.pallas_call(
        functools.partial(expert_kernel, capacity, ring),
        in_specs=[pl.BlockSpec(memory_space=pltpu.SMEM), ON_CHIP, ANYWHERE, ANYWHERE, ANYWHERE],
        out_specs=[ON_CHIP] * 4 + [ANYWHERE] * (2 * ring),
        out_shape=[
            pltpu.VMEM(gate.shape, BF16),
            pltpu.VMEM(up.shape, BF16),
            pltpu.VMEM((slots, 2 * hidden_size), BF16),
            pltpu.VMEM((slots, LANES), BF16),
        ]
        + [pltpu.HBM(block, BF16)] * (2 * ring),
        scratch_shapes=[
            pltpu.VMEM(down.shape, BF16),
            pltpu.VMEM((slots, features), BF16),
            pltpu.VMEM((slots, features), BF16),
            pltpu.VMEM((slots, hidden_size), BF16),
            pltpu.VMEM((2 * ring, *block), BF16),
            pltpu.SemaphoreType.DMA((3,)),
            pltpu.SemaphoreType.DMA((2 * ring,)),
        ],
        compiler_params=pltpu.CompilerParams(vmem_limit_bytes=28 * 2**20),
        name="expert_grads",
    )(place, *on_chip(received), *in_hbm(gate, up, down))


def return_kernel(capacity, inner_ref, score_ref, gate_ref, up_ref, out_ref):
    slots = inner_ref.shape[0]
    rows = out_ref.shape[0]
    hidden_size = gate_ref.shape[1]
    half = gate_ref.shape[0] // 2
    total = jnp.zeros((rows, half), F32)
    for part in range(2):
        piece = pl.ds(part * half, half)
        input_grad = dot(inner_ref[:, :hidden_size], gate_ref[piece, :], 1, 1) + dot(
            inner_ref[:, hidden_size:], up_ref[piece, :], 1, 1
        )
        spread = pick_rows(slots, rows, capacity, part)
        total += dot(spread, input_grad.astype(BF16), 0, 0)
        if part == 0:
            out_ref[:, half:] = dot(spread, score_ref[...], 0, 0).astype(BF16)
    out_ref[:, :half] = total.astype(BF16)


def return_rows(inner, score, gate, up, capacity):
    slots = inner.shape[0]
    half = gate.shape[0] // 2
    return pl.pallas_call(
        functools.partial(return_kernel, capacity),
        out_shape=jax.ShapeDtypeStruct((2 * slots, half + LANES), BF16),
        compiler_params=pltpu.CompilerParams(vmem_limit_bytes=24 * 2**20),
        name="return_rows",
    )(*on_chip(inner, score, gate, up))


def combine_kernel(capacity, ids_ref, slot_ref, score_ref, rows_ref, token_ref, grad_ref):
    rows = rows_ref.shape[0]
    count = token_ref.shape[0]
    half = token_ref.shape[1] // 2
    position = ids_ref[...] * (2 * capacity) + slot_ref[...]
    row = lax.broadcasted_iota(jnp.int32, (rows, count), 0)
    for part in range(2):
        pick = jnp.where(row == position + part * capacity, F32(1), F32(0)).astype(BF16)
        token_ref[:, part * half : (part + 1) * half] = dot(
            pick, rows_ref[:, :half], 0, 0
        ).astype(BF16)
        if part == 0:
            score = dot(rows_ref[:, half:], pick, 0, 0)
            grad_ref[...] = (score[0:1, :] / score_ref[...].astype(F32)).astype(BF16)


def combine(expert_ids, slot_index, gate_scores, rows, features, capacity):
    count = expert_ids.shape[0]
    return pl.pallas_call(
        functools.partial(combine_kernel, capacity),
        out_shape=[
            jax.ShapeDtypeStruct((count, features), BF16),
            jax.ShapeDtypeStruct((1, count), BF16),
        ],
        compiler_params=pltpu.CompilerParams(vmem_limit_bytes=24 * 2**20),
        name="combine",
    )(
        *in_hbm(
            expert_ids.reshape(1, count),
            slot_index.reshape(1, count),
            gate_scores.reshape(1, count),
        ),
        *on_chip(rows),
    )


def add_kernel(*refs):
    total = refs[0][...].astype(F32)
    for ref in refs[1:-1]:
        total += ref[...].astype(F32)
    refs[-1][...] = total.astype(BF16)


def add(*arrays):
    return pl.pallas_call(
        add_kernel,
        in_specs=[ON_CHIP] * len(arrays),
        out_specs=ON_CHIP,
        out_shape=pltpu.VMEM(arrays[0].shape, BF16),
        compiler_params=pltpu.CompilerParams(vmem_limit_bytes=6 * 2**20),
        name="add",
    )(*on_chip(*arrays))


def split_kernel(own_ref, up_way_ref, down_way_ref, other_ref, gate_ref, up_ref, down_ref):
    hidden_size = gate_ref.shape[1]
    total = own_ref[...].astype(F32) + up_way_ref[...].astype(F32)
    total += down_way_ref[...].astype(F32) + other_ref[...].astype(F32)
    gate_ref[...] = total[:, :hidden_size].astype(BF16)
    up_ref[...] = total[:, hidden_size : 2 * hidden_size].astype(BF16)
    down_ref[...] = total[:, 2 * hidden_size :].T.astype(BF16)


def split_grads(*parts):
    block, width = parts[0].shape
    hidden_size = width // 3
    return pl.pallas_call(
        split_kernel,
        in_specs=[ON_CHIP] * 4,
        out_shape=[
            jax.ShapeDtypeStruct((block, hidden_size), BF16),
            jax.ShapeDtypeStruct((block, hidden_size), BF16),
            jax.ShapeDtypeStruct((hidden_size, block), BF16),
        ],
        name="split_grads",
    )(*on_chip(*parts))


def ring_sums(grads, ring):
    far = ring // 2
    moves = {
        way: [(s * ring + i, s * ring + (i + way) % ring) for s in range(2) for i in range(ring)]
        for way in (1, -1)
    }
    block = lambda ahead, piece: grads[2 * (ahead % ring) + piece]
    carried = {}
    for hop in range(far, 0, -1):
        for piece in range(2):
            for way in (1, -1):
                if hop == far and piece != (0 if way == 1 else 1):
                    continue
                own = block(way * hop, piece)
                if (way, piece) in carried:
                    own = add(own, carried[way, piece])
                carried[way, piece] = lax.ppermute(own, "dp", moves[way])
    return [
        (block(0, piece), carried[1, piece], carried[-1, piece]) for piece in range(2)
    ]


def on_device(
    tokens, cotangent, gate_scores, expert_ids, slot_index, gate_weight, up_weight, down_weight
):
    experts = lax.axis_size("expert")
    count, features = tokens.shape
    capacity = 2 * count // experts
    gate, up, down = gate_weight[0], up_weight[0], down_weight[0]
    send = dispatch(expert_ids, slot_index, gate_scores, tokens, cotangent, experts, capacity)
    received = lax.all_to_all(
        send.reshape(experts, 2 * capacity, features),
        "expert", split_axis=0, concat_axis=0, tiled=True,
    ).reshape(send.shape)
    ring = lax.axis_size("dp") // 2
    index = lax.axis_index("dp")
    side = (index >= ring).astype(jnp.int32)
    place = jnp.stack([side, index - side * ring])
    gate, up, inner, score, *grads = expert_grads(place, ring, received, gate, up, down, capacity)
    back = return_rows(inner, score, gate, up, capacity)
    returned = lax.all_to_all(
        back.reshape(experts, 2 * capacity, back.shape[1]),
        "expert", split_axis=0, concat_axis=0, tiled=True,
    ).reshape(back.shape)
    for_other, kept = ring_sums(grads, ring)
    other = lax.ppermute(
        add(*for_other), "dp", [(i, (i + ring) % (2 * ring)) for i in range(2 * ring)]
    )
    token_grad, score_grad = combine(
        expert_ids, slot_index, gate_scores, returned, features, capacity
    )
    other, score_grad = lax.optimization_barrier((other, score_grad))
    grad_gate, grad_up, grad_down = split_grads(*kept, other)
    return token_grad, score_grad.reshape(count), grad_gate[None], grad_up[None], grad_down[None]


def solution(mesh):
    both = ("expert", "dp")
    return jax.shard_map(
        on_device,
        mesh=mesh,
        in_specs=(
            P(both, None),
            P(both, None),
            P(both),
            P(both),
            P(both),
            P("expert", None, None),
            P("expert", None, None),
            P("expert", None, None),
        ),
        out_specs=(
            P(both, None),
            P(both),
            P("expert", "dp", None),
            P("expert", "dp", None),
            P("expert", None, "dp"),
        ),
        check_vma=False,
    )
```
